32 devices in a mesh: dp: 4 (over z), shard: 8 (over y, x, core).
Axes of the slice: x: 2, y: 2, z: 4, core: 2. Of those that a mesh axis runs over, the one named last changes fastest.
Arguments:
- tokens_in: bfloat16 [2, 3072, 1536], P(None, ('dp', 'shard')), may hold values from -6 to 6
- in_weight: bfloat16 [1536, 4608], P(('dp', 'shard')), may hold values from -0.15625 to 0.15625
- conv_weight: bfloat16 [1536, 3], P(('dp', 'shard')), may hold values from -3.5 to 3.5
- out_weight: bfloat16 [1536, 1536], P(('dp', 'shard')), may hold values from -0.15625 to 0.15625
- norm_gain: bfloat16 [1536], P(('dp', 'shard')), may hold values from 0.25 to 1.75
- ff_gain: bfloat16 [1536], P(('dp', 'shard')), may hold values from 0.25 to 1.75
- gate_weight: bfloat16 [1536, 6912], P(('dp', 'shard')), may hold values from -0.15625 to 0.15625
- up_weight: bfloat16 [1536, 6912], P(('dp', 'shard')), may hold values from -0.15625 to 0.15625
- down_weight: bfloat16 [1536, 6912], P(('dp', 'shard')), may hold values from -0.078125 to 0.078125
- cotangent: bfloat16 [2, 3072, 1536], P(None, ('dp', 'shard')), may hold values from -6 to 6
- deal_table: int32 [2, 4, 8, 8], P(None, 'dp', 'shard'), may hold values from 0 to 7, each once within a row
- seq_lengths: int32 [2, 4, 3], P(None, 'dp'), may hold values from 1 to 720, 768 in all within a row
Outputs:
- block_out: bfloat16 [2, 3072, 1536], P(None, ('dp', 'shard'))
- tokens_grad: bfloat16 [2, 3072, 1536], P(None, ('dp', 'shard'))
- in_grad: float32 [1536, 4608], P(('dp', 'shard'))
- conv_grad: float32 [1536, 3], P(('dp', 'shard'))
- out_grad: float32 [1536, 1536], P(('dp', 'shard'))
- norm_gain_grad: float32 [1536], P(('dp', 'shard'))
- ff_gain_grad: float32 [1536], P(('dp', 'shard'))
- gate_grad: float32 [1536, 6912], P(('dp', 'shard'))
- up_grad: float32 [1536, 6912], P(('dp', 'shard'))
- down_grad: float32 [1536, 6912], P(('dp', 'shard'))
The draws below stay inside these ranges and needn't reach their ends.
Inputs may be any that keep to these rules, and one draw needn't show every extreme that they name: Each row deal_table[m, g, j, :] is a permutation of the shard indices: natural piece i of shard device j of group g lies in slot j of shard device deal_table[m, g, j, i]. `seq_lengths`: each row holds 3 lengths summing to 768, the largest exactly 720.
All inputs are finite; a program needn't handle non-finite values.
Results may differ from the reference program's by a relative error of at most 0.015.
Values may be sent and summed in bfloat16 or wider, within the bound.
No kernel may reach another device: no remote copies, remote signals or barrier semaphores. Data moves between devices by JAX's collectives and lax.ppermute only.
A program may use at most 384 MiB of HBM per device.

```python
import math
import jax
import jax.numpy as jnp
import numpy as np
from jax import lax

D = 1536
FF = 6912
KERNEL = 3
MB = 2
NSEQ = 3
PIECE = 12
GROUP_TOK = 768
TOKENS_MB = 3072
MAXLEN = 720
N_DP = 4
N_SHARD = 8


def raised(array, own_key, source, target, blocks, factor):
    owner, partner = [(jnp.arange(array.shape[dim]) // (array.shape[dim] // blocks)).reshape([-1 if axis == dim else 1 for axis in range(array.ndim)]) for dim in (source, target)]
    chosen = jax.random.permutation(own_key, blocks)[partner]
    strong = (owner == chosen) | (owner == (partner + blocks // 2) % blocks)
    return jnp.where(strong, factor * array, array)


def shard_levels(key, extent, split, least, high):
    level = 1.0
    for position, blocks in split:
        draws = jax.random.uniform(jax.random.fold_in(jax.random.fold_in(key, 6), position), (blocks,), jnp.float32, least / len(split), high / len(split))
        level = level * jnp.repeat(jnp.exp(draws), extent[position] // blocks).reshape((-1,) + (1,) * (len(extent) - 1 - position))
    return level


def split_up(amount, total, reach, lean):
    loads = [(1 << 20) // math.isqrt(grade ** lean) + 1 for grade in range(2, amount + 1)]
    surplus, holding = total - reach - (amount - 1), [1] * (amount - 1)
    while surplus > 0:
        free = [i for i in range(amount - 1) if holding[i] < reach]
        whole, remaining = sum([loads[i] for i in free]), surplus
        for i in free:
            addition = min(reach - holding[i], max(1, remaining * loads[i] // whole), surplus)
            holding[i] = holding[i] + addition
            surplus = surplus - addition
    return np.array([reach] + holding)


def uneven(rng, count, total, reach, slope):
    if count == 2:
        one = jax.random.randint(rng, (), max(1, total - reach), min(reach, total - 1) + 1)
        return jnp.stack([one, total - one])
    sizes = jnp.asarray(split_up(count, total, reach, slope), jnp.int32)
    couples = (count - 1) // 2
    donor, sink = sizes[1:1 + 2 * couples:2], sizes[2:2 + 2 * couples:2]
    margin = jnp.minimum(donor - 1, reach - sink)
    passed = jax.random.randint(jax.random.fold_in(rng, 1), (couples,), 0, 1 << 20) % (margin + 1)
    sizes = sizes.at[1:1 + 2 * couples:2].set(donor - passed).at[2:2 + 2 * couples:2].set(sink + passed)
    return sizes[jax.random.permutation(jax.random.fold_in(rng, 2), count)]


def scatter_about(key, extent, deviation, reach, shards=(), held_as=jnp.bfloat16):
    loudness = shard_levels(key, extent, shards, -0.22, 0.18) if shards else 1.0
    values = jax.random.normal(key, extent, jnp.float32) * deviation * loudness
    return jnp.minimum(jnp.maximum(values, -reach), reach).astype(held_as)


def gaussian_with(stream_key, dims, width, most, split, heavy, held_as=jnp.bfloat16):
    drawn = width * jax.random.normal(stream_key, dims, jnp.float32)
    if split:
        drawn = drawn * shard_levels(stream_key, dims, split, -0.22, 0.18)
    return jnp.clip(raised(drawn, jax.random.fold_in(stream_key, 3), *heavy), -most, most).astype(held_as)


def setup_inputs(seed: int = 0) -> dict:
    keys = jax.random.split(jax.random.key(seed), 13)
    tokens_in = gaussian_with(keys[0], (MB, TOKENS_MB, D), 1.0, 6.0, ((1, 32),), (1, 2, 32, 2.75))
    in_weight = scatter_about(keys[1], (D, 3 * D), D ** -0.5, 0.15625, ((0, 32),))
    conv_weight = scatter_about(keys[2], (D, KERNEL), KERNEL ** -0.5, 3.5, ((0, 32),))
    out_weight = scatter_about(keys[3], (D, D), D ** -0.5, 0.15625, ((0, 32),))
    norm_gain = jnp.clip(1.0 + 0.15 * jax.random.normal(keys[4], (D,), jnp.float32), 0.25, 1.75).astype(jnp.bfloat16)
    ff_gain = jnp.clip(1.0 + 0.15 * jax.random.normal(keys[5], (D,), jnp.float32), 0.25, 1.75).astype(jnp.bfloat16)
    gate_weight = scatter_about(keys[6], (D, FF), D ** -0.5, 0.15625, ((0, 32),))
    up_weight = scatter_about(keys[7], (D, FF), D ** -0.5, 0.15625, ((0, 32),))
    down_weight = scatter_about(keys[8], (D, FF), FF ** -0.5, 0.078125, ((0, 32),))
    cotangent = gaussian_with(keys[9], (MB, TOKENS_MB, D), 1.0, 6.0, ((1, 32),), (1, 2, 32, 2.75))
    deal_table = jax.vmap(lambda own: jax.random.permutation(own, N_SHARD))(jax.random.split(keys[10], MB * N_DP * N_SHARD)).reshape((MB, N_DP, N_SHARD, N_SHARD)).astype(jnp.int32)
    seq_lengths = jax.vmap(lambda own: uneven(own, NSEQ, GROUP_TOK, MAXLEN, 2))(jax.random.split(keys[11], MB * N_DP)).reshape((MB, N_DP, NSEQ)).astype(jnp.int32)
    return dict(tokens_in=tokens_in, in_weight=in_weight, conv_weight=conv_weight, out_weight=out_weight, norm_gain=norm_gain, ff_gain=ff_gain, gate_weight=gate_weight, up_weight=up_weight, down_weight=down_weight, cotangent=cotangent, deal_table=deal_table, seq_lengths=seq_lengths)


EPS = 1e-05

@jax.custom_vjp
def low(v):
    return lax.optimization_barrier(v.astype(jnp.bfloat16)).astype(jnp.float32)

@jax.custom_vjp
def low_back(v):
    return v

def low_keep(v):
    return (low(v), None)

def low_pass(kept, grad):
    return (grad,)

def back_keep(v):
    return (v, None)

def back_low(kept, grad):
    return (low(grad),)
low.defvjp(low_keep, low_pass)
low_back.defvjp(back_keep, back_low)

def matmul(former, latter):
    return jnp.dot(former, latter, precision=lax.Precision.HIGHEST)

def times_trans(former, latter):
    return lax.dot_general(former, latter, (((1,), (1,)), ((), ())), precision=lax.Precision.HIGHEST)

def rms_norm(values, gain_vec):
    return values * lax.rsqrt(lax.optimization_barrier(jnp.mean(values * values, axis=-1, keepdims=True)) + EPS) * gain_vec

def layer(tokens, in_w, conv_w, out_w, gain_one, gain_two, gate_w, up_w, down_w, after_one, after_two):
    normed = low(rms_norm(tokens, gain_one))
    projected = low_back(matmul(normed, in_w))
    b_part = projected[:, :D]
    c_part = projected[:, D:2 * D]
    x_part = projected[:, 2 * D:]
    product = low_back(low(b_part * x_part))
    prev_one = jnp.concatenate([jnp.zeros((1, D), product.dtype), product[:-1]], 0) * after_one[:, None]
    prev_two = jnp.concatenate([jnp.zeros((2, D), product.dtype), product[:-2]], 0) * after_two[:, None]
    conv_out = prev_two * conv_w[:, 0] + prev_one * conv_w[:, 1] + product * conv_w[:, 2]
    gated_mix = low(c_part * conv_out)
    hidden = tokens + low_back(matmul(gated_mix, out_w))
    normed_ff = low(rms_norm(hidden, gain_two))
    gate_val = low_back(matmul(normed_ff, gate_w))
    up_val = low_back(matmul(normed_ff, up_w))
    ff_inner = low(jax.nn.silu(gate_val) * up_val)
    return hidden + times_trans(ff_inner, down_w)

def to_natural(dealt_tok, deal_rows):
    pieces = dealt_tok.reshape(N_DP, N_SHARD, N_SHARD, PIECE, D).transpose(0, 2, 1, 3, 4)
    picked = pieces[jnp.arange(N_DP)[:, None, None], jnp.arange(N_SHARD)[None, :, None], deal_rows]
    return picked.reshape(N_DP, GROUP_TOK, D)

def to_dealt(natural, deal_rows):
    pieces = natural.reshape(N_DP, N_SHARD, N_SHARD, PIECE, D)
    inverse = jnp.argsort(deal_rows, axis=-1).astype(jnp.int32)
    picked = pieces[jnp.arange(N_DP)[:, None, None], jnp.arange(N_SHARD)[None, :, None], inverse]
    return picked.transpose(0, 2, 1, 3, 4).reshape(N_DP * GROUP_TOK, D)

def positions(lengths):
    starts = (jnp.cumsum(lengths) - lengths).astype(jnp.int32)
    places = jnp.arange(GROUP_TOK, dtype=jnp.int32)
    seq_start = lax.optimization_barrier(jnp.max(jnp.where(starts[None, :] <= places[:, None], starts[None, :], 0), axis=1))
    return (places - seq_start).astype(jnp.int32)

def reference(tokens_in, in_weight, conv_weight, out_weight, norm_gain, ff_gain, gate_weight, up_weight, down_weight, cotangent, deal_table, seq_lengths):
    weights = tuple((item.astype(jnp.float32) for item in (in_weight, conv_weight, out_weight, norm_gain, ff_gain, gate_weight, up_weight, down_weight)))
    groups_tok = jnp.concatenate([to_natural(tokens_in[which_batch], deal_table[which_batch]) for which_batch in range(MB)], 0)
    groups_cot = cotangent.reshape(MB * N_DP, GROUP_TOK, D)
    places = jax.vmap(positions)(seq_lengths.reshape(MB * N_DP, NSEQ))

    def one_group(totals, inputs):
        tok_group, cot_group, place_group = inputs
        after_one = (place_group >= 1).astype(jnp.float32)
        after_two = (place_group >= 2).astype(jnp.float32)

        def forward(tok_vals, *params):
            return layer(tok_vals, *params, after_one, after_two)
        result, pullback = jax.vjp(forward, tok_group.astype(jnp.float32), *weights)
        gradients = pullback(cot_group.astype(jnp.float32))
        totals = jax.tree.map(jnp.add, totals, tuple(gradients[1:]))
        return (totals, (result.astype(jnp.bfloat16), gradients[0].astype(jnp.bfloat16)))
    zeros_init = tuple((jnp.zeros_like(item) for item in weights))
    totals, outputs = lax.scan(one_group, zeros_init, (groups_tok, groups_cot, places))
    block_out = outputs[0].reshape(MB, TOKENS_MB, D)
    back_groups = outputs[1]
    tokens_grad = jnp.stack([to_dealt(back_groups[which_batch * N_DP:(which_batch + 1) * N_DP], deal_table[which_batch]) for which_batch in range(MB)], 0)
    return (block_out, tokens_grad, totals[0], totals[1], totals[2], totals[3], totals[4], totals[5], totals[6], totals[7])
```

```python
import jax
import jax.numpy as jnp
from jax import lax
from jax.sharding import PartitionSpec as P

EPS = 1e-05
F32 = jnp.float32
BF16 = jnp.bfloat16
LANES = 128


def dot(former, latter, dims, out=F32):
    return lax.dot_general(
        former, latter, ((dims[0], dims[1]), ((), ())), preferred_element_type=F32
    ).astype(out)


def bits_of(count):
    return [1 << k for k in range(count.bit_length() - 1)]


def swap(value, bit):
    n = lax.axis_size("shard")
    return lax.ppermute(value, "shard", [(i, i ^ bit) for i in range(n)])


def route(outer, turn):
    turn = turn % len(outer)
    return outer[turn:] + outer[:turn]


def last_of(index, order):
    return [bit for bit in order if index & bit][-1]


def by_count(n):
    return sorted(range(1, n), key=lambda index: (bin(index).count("1"), index))


def plane_gather(parts):
    n = lax.axis_size("shard")
    outer = bits_of(n)[1:]
    near = []
    for turn, part in enumerate(parts):
        order = route(outer, turn)
        held = {0: part}
        for e in by_count(n // 2):
            bit = last_of(2 * e, order)
            held[e] = swap(held[e ^ (bit >> 1)], bit)
        near.append([held[e] for e in range(n // 2)])
    far = [[swap(block, 1) for block in blocks] for blocks in near]
    return jnp.stack([jnp.stack([jnp.stack(b) for b in half]) for half in (near, far)])


def plane_reduce(near, far):
    n = lax.axis_size("shard")
    outer = bits_of(n)[1:]
    sums = []
    for turn in range(near.shape[0]):
        order = route(outer, turn)
        came = swap(far[turn], 1)
        held = {e: near[turn, e] + came[e].astype(F32) for e in range(n // 2)}
        for e in reversed(by_count(n // 2)):
            bit = last_of(2 * e, order)
            held[e ^ (bit >> 1)] = held[e ^ (bit >> 1)] + swap(held[e].astype(BF16), bit).astype(F32)
        sums.append(held[0])
    return jnp.stack(sums)


def plane_deal(blocks, order):
    held = list(blocks)
    for bit in order:
        picked = [r for r in range(len(held)) if r & bit]
        came = swap(jnp.stack([held[r] for r in picked]), bit)
        for place, r in enumerate(picked):
            held[r] = came[place]
    return held


def line_gather(block):
    n = lax.axis_size("dp")
    z = lax.axis_index("dp")
    ups, downs = {0: block}, {0: block}
    for k in range(1, n):
        ups[k] = lax.ppermute(ups[k - 1], "dp", [(i, i + 1) for i in range(k - 1, n - 1)])
        downs[k] = lax.ppermute(downs[k - 1], "dp", [(i + 1, i) for i in range(n - k)])
    return [block] + [jnp.where(z + d < n, downs[d], ups[n - d]) for d in range(1, n)]


def line_reduce(terms):
    n = lax.axis_size("dp")
    up = down = None
    for d in range(n - 1, 0, -1):
        going = terms[d] if up is None else terms[d] + up.astype(F32)
        up = lax.ppermute(going.astype(BF16), "dp", [(i, i + 1) for i in range(n - d)])
        going = terms[n - d] if down is None else terms[n - d] + down.astype(F32)
        down = lax.ppermute(going.astype(BF16), "dp", [(i, i - 1) for i in range(d, n)])
    return terms[0] + up.astype(F32) + down.astype(F32)


def turned(value, blocks, amount):
    width = value.shape[-1] // blocks
    out = value
    for k in range(1, blocks):
        out = jnp.where(amount == k, jnp.roll(value, -k * width, axis=-1), out)
    return out


def xor_blocks(value, axis, n):
    index = lax.axis_index("shard")
    for bit in bits_of(n):
        shape = value.shape
        split = value.reshape(shape[:axis] + (n // (2 * bit), 2, bit) + shape[axis + 1 :])
        low = lax.slice_in_dim(split, 0, 1, axis=axis + 1)
        high = lax.slice_in_dim(split, 1, 2, axis=axis + 1)
        flipped = jnp.concatenate([high, low], axis=axis + 1)
        value = jnp.where((index & bit) != 0, flipped, split).reshape(shape)
    return value


def body(
    tokens_in,
    in_weight,
    conv_weight,
    out_weight,
    norm_gain,
    ff_gain,
    gate_weight,
    up_weight,
    down_weight,
    cotangent,
    deal_table,
    seq_lengths,
):
    batches, rows_dev, width = tokens_in.shape
    n, n_dp = lax.axis_size("shard"), lax.axis_size("dp")
    half = n // 2
    me, z = lax.axis_index("shard"), lax.axis_index("dp")
    group = n * rows_dev
    piece_rows = rows_dev // n
    own_rows, hidden_units = gate_weight.shape
    total = batches * group
    outer = bits_of(n)[1:]
    order_a, order_b = [1] + route(outer, 0), [1] + route(outer, 1)
    zblock = n * own_rows
    channels = n_dp * own_rows

    whole = hidden_units // (LANES * n) * LANES
    rest = hidden_units // n - whole

    def pick(stacked, r):
        return lax.dynamic_index_in_dim(stacked, me ^ r, 0, keepdims=False)

    def spread_columns(weight):
        return jnp.stack(
            [
                jnp.concatenate(
                    [
                        weight[:, s * whole : (s + 1) * whole],
                        weight[:, n * whole + s * rest : n * whole + (s + 1) * rest],
                    ],
                    axis=1,
                )
                for s in range(n)
            ]
        )

    def join_columns(blocks):
        return jnp.concatenate(
            [blocks[s, :, :whole] for s in range(n)] + [blocks[s, :, whole:] for s in range(n)],
            axis=1,
        )

    place = jnp.arange(zblock, dtype=jnp.int32)
    arrival = ((place // own_rows) ^ me) * own_rows + place % own_rows
    to_natural = (arrival[:, None] == place[None, :]).astype(BF16)

    def spread(stacked, order):
        came = plane_deal([pick(stacked, r) for r in range(n)], order)
        block = jnp.concatenate(came, axis=0)
        return dot(block, to_natural, ((0,), (0,)), BF16)

    def collect(summed, order):
        rows = dot(to_natural, summed.astype(BF16), ((1,), (1,)), BF16)
        rows = rows.reshape(n, own_rows, -1)
        came = plane_deal([rows[r] for r in range(n)], order)
        stacked = jnp.stack(came)
        return jnp.stack([pick(stacked, s) for s in range(n)])

    def line_matrix(block):
        return jnp.concatenate(line_gather(block), axis=1)

    tok_turned = turned(tokens_in, n_dp, z)
    tok_all = plane_gather([tok_turned[m] for m in range(batches)]).reshape(total, width)
    cot_turned = turned(cotangent, n_dp, z)
    cot_all = plane_gather([cot_turned[m] for m in range(batches)]).reshape(total, width)

    out_aug = jnp.concatenate(
        [out_weight, conv_weight, jnp.zeros((own_rows, LANES - conv_weight.shape[1]), BF16)], axis=1
    )
    out_lines = jnp.stack(line_gather(out_aug))
    in_parts = in_weight.reshape(own_rows, 3 * n_dp, n, own_rows).transpose(2, 0, 1, 3)
    in_parts = in_parts.reshape(n, own_rows, 3 * channels)
    gains = jnp.stack([norm_gain, ff_gain], axis=1)
    gain_cols = jnp.pad(gains, ((0, 0), (0, 14)))
    in_parts = jnp.concatenate(
        [in_parts, jnp.broadcast_to(gain_cols[None], (n,) + gain_cols.shape)], axis=2
    )
    in_full = line_matrix(spread(in_parts, order_b))
    gate_t = line_matrix(spread(spread_columns(gate_weight), order_a))
    up_t = line_matrix(spread(spread_columns(up_weight), order_b))
    down_t = line_matrix(spread(spread_columns(down_weight), order_a))
    in_t = in_full[: 3 * channels]
    gain_one = in_full[3 * channels].astype(F32)
    gain_two = turned(in_full[3 * channels + 1], n_dp, n_dp - z).astype(F32)
    natural_lines = out_lines[0][None]
    stacked_lines = jnp.stack(
        [lax.dynamic_index_in_dim(out_lines, (k - z) % n_dp, 0, keepdims=False) for k in range(n_dp)]
    ).reshape(channels, width + LANES)
    out_full = stacked_lines[:, :width]
    taps = stacked_lines[:, width : width + conv_weight.shape[1]].astype(F32).T

    table = deal_table[:, 0, 0, :].astype(F32)
    seen = table[None]
    for bit in bits_of(n):
        seen = jnp.concatenate([seen, swap(seen, bit)], axis=0)
    deal = xor_blocks(seen, 0, n).astype(jnp.int32)
    deal = deal.transpose(1, 0, 2)
    m_index = jnp.arange(batches, dtype=jnp.int32)[:, None, None, None]
    j_index = jnp.arange(n, dtype=jnp.int32)[None, :, None, None]
    i_index = jnp.arange(n, dtype=jnp.int32)[None, None, :, None]
    t_index = jnp.arange(piece_rows, dtype=jnp.int32)[None, None, None, :]

    def arrival_row(m, holder, row):
        rel = holder ^ me
        return (((rel & 1) * batches + m) * half + (rel >> 1)) * rows_dev + row

    source = arrival_row(m_index, deal[:, :, :, None], j_index * piece_rows + t_index)
    source = source.reshape(total)
    columns = jnp.arange(total, dtype=jnp.int32)
    deal_mat = (source[:, None] == columns[None, :]).astype(BF16)
    own_source = lax.dynamic_index_in_dim(source.reshape(batches, n, rows_dev), me, 1, keepdims=False)
    own_mat = (own_source.reshape(-1)[:, None] == columns[None, :]).astype(BF16)
    inverse = jnp.sum(jnp.where(deal == me, jnp.arange(n, dtype=jnp.int32)[None, None, :], 0), axis=2)
    slot_source = arrival_row(
        m_index[:, :, 0], j_index[:, :, 0], inverse[:, :, None] * piece_rows + t_index[:, 0]
    )
    slot_mat = (slot_source.reshape(-1)[:, None] == columns[None, :]).astype(BF16)

    lengths = seq_lengths[:, 0, :]
    places = jnp.arange(group, dtype=jnp.int32)
    seq_start = jnp.zeros((batches, group), jnp.int32)
    start = jnp.zeros((batches,), jnp.int32)
    for k in range(lengths.shape[1]):
        seq_start = jnp.where(start[:, None] <= places[None, :], start[:, None], seq_start)
        start = start + lengths[:, k]
    offset = places[None, :] - seq_start
    after_one = (offset >= 1).astype(F32)[:, :, None]
    after_two = (offset >= 2).astype(F32)[:, :, None]

    tok_wide = tok_all.astype(F32)
    unit = tok_wide * lax.rsqrt(jnp.mean(tok_wide * tok_wide, axis=1, keepdims=True) + EPS)
    normed = (unit * gain_one).astype(BF16)
    projected = dot(normed, in_t, ((1,), (1,)))
    b_part = projected[:, :channels]
    c_part = projected[:, channels : 2 * channels]
    x_part = projected[:, 2 * channels :]
    c_high = c_part.astype(BF16)
    c_low = (c_part - c_high.astype(F32)).astype(BF16)
    product = (b_part * x_part).astype(BF16)
    moved = dot(deal_mat, jnp.concatenate([product, c_high, c_low], axis=1), ((1,), (0,)))
    moved = moved.reshape(batches, group, 3 * channels)
    product_nat = moved[:, :, :channels]
    c_nat = moved[:, :, channels : 2 * channels] + moved[:, :, 2 * channels :]
    zero_row = jnp.zeros((batches, 1, channels), F32)
    shift_one = jnp.concatenate([zero_row, product_nat[:, :-1]], axis=1)
    shift_two = jnp.concatenate([zero_row, zero_row, product_nat[:, :-2]], axis=1)
    prev_one = shift_one * after_one
    prev_two = shift_two * after_two
    conv_out = prev_two * taps[0] + prev_one * taps[1] + product_nat * taps[2]
    gated = (c_nat * conv_out).astype(BF16)

    def to_arrival(value):
        k = value.shape[-1]
        blocks = xor_blocks(value.reshape(batches, n, rows_dev, k), 1, n)
        blocks = blocks.reshape(batches, half, 2, rows_dev, k).transpose(2, 0, 1, 3, 4)
        return blocks.reshape(total, k)

    def from_arrival(value):
        k = value.shape[-1]
        blocks = value.reshape(2, batches, half, rows_dev, k).transpose(1, 2, 0, 3, 4)
        return xor_blocks(blocks.reshape(batches, n, rows_dev, k), 1, n).reshape(batches, group, k)

    def summed_rows(pairs):
        far = sum(dot(a[total // 2 :], b, ((1,), (0,))) for a, b in pairs).astype(BF16)
        near = sum(dot(a[: total // 2], b, ((1,), (0,))) for a, b in pairs)
        shape = (batches, half, rows_dev, width)
        return plane_reduce(near.reshape(shape), far.reshape(shape))

    gated_arr = to_arrival(gated)
    own_tok = turned(dot(own_mat, tok_all, ((1,), (0,))), n_dp, n_dp - z)
    own_tok = own_tok.reshape(batches, rows_dev, width)
    hidden = own_tok + summed_rows([(gated_arr, out_full)])
    inv_two = lax.rsqrt(jnp.mean(hidden * hidden, axis=2, keepdims=True) + EPS)
    unit_two = hidden * inv_two
    ff_own = turned((unit_two * gain_two).astype(BF16), n_dp, z)
    normed_ff = plane_gather([ff_own[m] for m in range(batches)]).reshape(total, width)

    gate_val = dot(normed_ff, gate_t, ((1,), (1,)))
    up_val = dot(normed_ff, up_t, ((1,), (1,)))
    sigmoid_val = jax.nn.sigmoid(gate_val)
    silu_val = gate_val * sigmoid_val
    ff_inner = (silu_val * up_val).astype(BF16)
    d_inner = dot(cot_all, down_t, ((1,), (1,)))
    silu_slope = sigmoid_val * (1.0 + gate_val * (1.0 - sigmoid_val))
    d_gate = (d_inner * up_val * silu_slope).astype(BF16)
    d_up = (d_inner * silu_val).astype(BF16)
    d_ff = turned(summed_rows([(d_gate, gate_t), (d_up, up_t)]), n_dp, n_dp - z)
    cot_wide = cotangent.astype(F32)
    scaled_ff = d_ff * gain_two
    d_hidden = cot_wide + inv_two * (
        scaled_ff - unit_two * jnp.mean(scaled_ff * unit_two, axis=2, keepdims=True)
    )
    branch_own = d_hidden.astype(BF16)
    branch = plane_gather([branch_own[m] for m in range(batches)]).reshape(total, width)
    block_val = turned(summed_rows([(ff_inner, down_t)]), n_dp, n_dp - z)
    block_out = (hidden + block_val).astype(BF16)

    d_gated = from_arrival(dot(branch, out_full, ((1,), (1,))))
    grad_c = (d_gated * conv_out).astype(BF16)
    grad_conv = d_gated * c_nat
    from_one = grad_conv * after_one * taps[1]
    from_two = grad_conv * after_two * taps[0]
    d_product = (
        grad_conv * taps[2]
        + jnp.concatenate([from_one[:, 1:], zero_row], axis=1)
        + jnp.concatenate([from_two[:, 2:], zero_row, zero_row], axis=1)
    ).astype(BF16)
    back = jnp.concatenate([d_product, grad_c], axis=2).reshape(total, 2 * channels)
    back = dot(deal_mat, back, ((0,), (0,)))
    d_prod_arr = back[:, :channels]
    grad_proj = jnp.concatenate(
        [d_prod_arr * x_part, back[:, channels:], d_prod_arr * b_part], axis=1
    ).astype(BF16)
    d_normed = turned(summed_rows([(grad_proj, in_t)]), n_dp, n_dp - z)
    own_wide = tokens_in.astype(F32)
    inv_one = lax.rsqrt(jnp.mean(own_wide * own_wide, axis=2, keepdims=True) + EPS)
    unit_own = own_wide * inv_one
    gain_nat = turned(in_full[3 * channels], n_dp, n_dp - z).astype(F32)
    scaled_one = d_normed * gain_nat
    d_hidden_own = dot(slot_mat, branch, ((1,), (0,))).reshape(batches, rows_dev, width)
    tokens_grad = (
        d_hidden_own
        + inv_one * (scaled_one - unit_own * jnp.mean(scaled_one * unit_own, axis=2, keepdims=True))
    ).astype(BF16)

    def summed_matrix(grad):
        step = width // n_dp
        return line_reduce([grad[:, d * step : (d + 1) * step] for d in range(n_dp)])

    down_sum = summed_matrix(dot(ff_inner, cot_all, ((0,), (0,))))
    gate_sum = summed_matrix(dot(d_gate, normed_ff, ((0,), (0,))))
    up_sum = summed_matrix(dot(d_up, normed_ff, ((0,), (0,))))
    in_sum = summed_matrix(dot(grad_proj, normed, ((0,), (0,))))
    out_term = dot(gated_arr, branch, ((0,), (0,)))
    conv_term = jnp.stack(
        [
            jnp.sum(grad_conv * tap_in, axis=(0, 1))
            for tap_in in (prev_two, prev_one, product_nat)
        ],
        axis=1,
    )
    out_term = jnp.concatenate(
        [out_term, conv_term, jnp.zeros((channels, LANES - conv_term.shape[1]), F32)], axis=1
    ).reshape(n_dp, own_rows, width + LANES)
    out_sum = line_reduce(
        [
            lax.dynamic_index_in_dim(out_term, (z + d) % n_dp, 0, keepdims=False)
            for d in range(n_dp)
        ]
    )
    out_grad = out_sum[:, :width]
    conv_grad = out_sum[:, width : width + conv_weight.shape[1]]
    down_grad = join_columns(collect(down_sum, order_a)).astype(F32)
    gate_grad = join_columns(collect(gate_sum, order_b)).astype(F32)
    up_grad = join_columns(collect(up_sum, order_a)).astype(F32)
    in_blocks = collect(in_sum, order_b).reshape(n, own_rows, 3 * n_dp, own_rows)
    in_grad = in_blocks.transpose(1, 2, 0, 3).reshape(own_rows, 3 * width).astype(F32)
    norm_gain_grad = jnp.sum(in_weight.astype(F32) * in_grad, axis=1) / norm_gain.astype(F32)
    ff_gain_grad = (
        jnp.sum(gate_weight.astype(F32) * gate_grad, axis=1)
        + jnp.sum(up_weight.astype(F32) * up_grad, axis=1)
    ) / ff_gain.astype(F32)
    return (
        block_out,
        tokens_grad,
        in_grad,
        conv_grad,
        out_grad,
        norm_gain_grad,
        ff_gain_grad,
        gate_grad,
        up_grad,
        down_grad,
    )


def solution(mesh):
    rows = P(("dp", "shard"), None)
    tokens = P(None, ("dp", "shard"), None)
    vector = P(("dp", "shard"))
    placed = (
        tokens,
        rows,
        rows,
        rows,
        vector,
        vector,
        rows,
        rows,
        rows,
        tokens,
        P(None, "dp", "shard", None),
        P(None, "dp", None),
    )
    return jax.shard_map(
        body,
        mesh=mesh,
        in_specs=placed,
        out_specs=(tokens, tokens, rows, rows, rows, vector, vector, rows, rows, rows),
        check_vma=False,
    )
```

```python
import functools

import jax
import jax.numpy as jnp
from jax import lax
from jax.experimental import pallas as pl
from jax.experimental.pallas import tpu as pltpu
from jax.sharding import PartitionSpec as P

EPS = 1e-05
F32 = jnp.float32
BF16 = jnp.bfloat16
LANES = 128


def dot(former, latter, dims, out=F32):
    return lax.dot_general(
        former, latter, ((dims[0], dims[1]), ((), ())), preferred_element_type=F32
    ).astype(out)


def bits_of(count):
    return [1 << k for k in range(count.bit_length() - 1)]


def swap(value, bit, axis="shard"):
    n = lax.axis_size(axis)
    return lax.ppermute(value, axis, [(i, i ^ bit) for i in range(n)])


def route(outer, turn):
    turn = turn % len(outer)
    return outer[turn:] + outer[:turn]


def after(value, *others):
    others = [other for other in others if other is not None]
    if not others:
        return value
    return lax.optimization_barrier((value, *others))[0]


def gather_names(n, parts):
    outer = bits_of(n)[1:]
    names = []
    for m in range(parts):
        order = [0]
        for bit in route(outer, m):
            order = order + [e ^ (bit >> 1) for e in order]
        names.append(order)
    return names


def plane_gather(parts, waits=((), ())):
    n = lax.axis_size("shard")
    outer = bits_of(n)[1:]
    held = [[part] for part in parts]
    steps = []
    for k in range(len(outer)):
        going = [h[0] if len(h) == 1 else jnp.concatenate(h, axis=0) for h in held]
        if k < len(waits):
            going = [after(g, *waits[k]) for g in going]
        came = [swap(going[m], route(outer, m)[k]) for m in range(len(parts))]
        held = [[g, c] for g, c in zip(going, came)]
        steps.append(tuple(came))
    near = [piece for h in held for piece in h]
    far = [swap(piece, 1) for piece in near]
    return near + far, steps


def fold_kernel(rows, plans, *refs):
    count = len(plans)
    kept, came, sends, keeps = (refs[k * count : (k + 1) * count] for k in range(4))
    for m, (going, staying) in enumerate(plans):
        for out, places in ((sends[m], going), (keeps[m], staying)):
            for k, place in enumerate(places):
                at = slice(place * rows, (place + 1) * rows)
                value = kept[m][at, :] + came[m][at, :].astype(F32)
                out[k * rows : (k + 1) * rows, :] = value.astype(out.dtype)


def first_fold_kernel(rows, plans, near, came, *refs):
    count = len(plans)
    sends, keeps = refs[:count], refs[count:]
    for m, (going, staying) in enumerate(plans):
        for out, places in ((sends[m], going), (keeps[m], staying)):
            for k, place in enumerate(places):
                at = slice(place * rows, (place + 1) * rows)
                value = near[at, :] + came[at, :].astype(F32)
                out[k * rows : (k + 1) * rows, :] = value.astype(out.dtype)


def plane_reduce(near, far, parts, wait=()):
    n = lax.axis_size("shard")
    half = n // 2
    outer = bits_of(n)[1:]
    width = near.shape[1]
    rows = near.shape[0] // (parts * half)
    came = swap(far, 1)
    names = gather_names(n, parts)
    kept, arrived = near, came
    for k in reversed(range(len(outer))):
        plans = []
        for m in range(parts):
            bit = route(outer, m)[k] >> 1
            going = [e for e in names[m] if e & bit]
            base = m * half if kept is near else 0
            plans.append(([base + names[m].index(e) for e in going], [base + names[m].index(e ^ bit) for e in going]))
            names[m] = [e ^ bit for e in going]
        shape = (len(plans[0][0]) * rows, width)
        outs = [(shape, BF16)] * parts + [(shape, F32)] * parts
        if kept is near:
            made = run(functools.partial(first_fold_kernel, rows, plans), outs, [], [near, came])
            sends = [after(send, *wait) for send in made[:parts]]
        else:
            made = run(functools.partial(fold_kernel, rows, plans), outs, [], [*kept, *arrived])
            sends = made[:parts]
        kept = made[parts:]
        arrived = [swap(sends[m], route(outer, m)[k]) for m in range(parts)]
    return [*kept, *arrived]


def line_gather(block, wait=None):
    n = lax.axis_size("dp")
    block = after(block, *(wait or ()))
    ready = None
    for bit in reversed(bits_of(n)):
        came = swap(block, bit, "dp")
        ready = (came,) if ready is None else ready
        if bit == 1:
            return block, came, ready
        block = jnp.concatenate([block, came], axis=1)


def line_reduce(keep, send, wait=None):
    n = lax.axis_size("dp")
    ready = None
    send = after(send, *(wait or ()))
    for bit in bits_of(n):
        came = swap(send, bit, "dp")
        ready = (came,) if ready is None else ready
        if 2 * bit == n:
            return keep, came, ready
        total = keep + came.astype(F32)
        cut = total.shape[1] // 2
        keep, send = total[:, :cut], total[:, cut:].astype(BF16)


def reversed_bits(index, n):
    out = 0
    for k, bit in enumerate(bits_of(n)):
        if index & bit:
            out |= n >> (k + 1)
    return out


def turned(value, z, n):
    step = value.shape[-1] // n
    pieces = [value[..., k * step : (k + 1) * step] for k in range(n)]
    out = None
    for k in range(n):
        order = [pieces[k ^ reversed_bits(p, n)] for p in range(n)]
        moved = jnp.concatenate(order, axis=-1)
        out = moved if out is None else jnp.where(z == k, moved, out)
    return out


def exchange(value, z, n, back):
    step = value.shape[1] // n
    pieces = [value[:, p * step : (p + 1) * step] for p in range(n)]

    def reorder(pieces):
        return [pieces[reversed_bits(p, n)] for p in range(n)]

    def flip(pieces):
        for k, bit in enumerate(bits_of(n)):
            low = n >> (k + 1)
            pieces = [jnp.where((z & bit) != 0, pieces[p ^ low], pieces[p]) for p in range(n)]
        return pieces

    return jnp.concatenate(reorder(flip(pieces)) if back else flip(reorder(pieces)), axis=1)


WHOLE = pl.BlockSpec(memory_space=pltpu.VMEM)
SCALAR = pl.BlockSpec(memory_space=pltpu.SMEM)


def run(kernel, outs, scalars, arrays, scratch=()):
    return pl.pallas_call(
        kernel,
        out_shape=[jax.ShapeDtypeStruct(shape, dtype) for shape, dtype in outs],
        in_specs=[SCALAR] * len(scalars) + [WHOLE] * len(arrays),
        out_specs=[WHOLE] * len(outs),
        scratch_shapes=list(scratch),
        compiler_params=pltpu.CompilerParams(vmem_limit_bytes=48 * 2**20),
        cost_estimate=pl.CostEstimate(flops=1000, bytes_accessed=1000, transcendentals=0),
    )(*[jnp.asarray(v, jnp.int32).reshape(1) for v in scalars], *arrays)


def mm(former, latter):
    return lax.dot_general(former, latter, (((1,), (0,)), ((), ())), preferred_element_type=F32)


def mt(former, latter):
    return lax.dot_general(former, latter, (((1,), (1,)), ((), ())), preferred_element_type=F32)


def spread_kernel(n, whole, rest, count, *refs):
    weights, out = refs[:count], refs[count]
    rows = weights[0].shape[0]
    for k in range(count):
        for s in range(n):
            at = slice(k * rows, (k + 1) * rows)
            first = n * whole + s * rest
            out[s, at, :whole] = weights[k][:, s * whole : (s + 1) * whole]
            out[s, at, whole:] = weights[k][:, first : first + rest]


def join_kernel(n, whole, rest, came, weight, grad, dots):
    grad[:, n * whole :] = jnp.concatenate([came[s, :, whole:] for s in range(n)], axis=1).astype(F32)
    for s in range(n):
        grad[:, s * whole : (s + 1) * whole] = came[s, :, :whole].astype(F32)
    dots[...] = jnp.sum(grad[...] * weight[...].astype(F32), axis=1, keepdims=True)


def join_in_kernel(n, groups, came, weight, grad, dots):
    rows = came.shape[1]
    for g in range(groups):
        piece = jnp.concatenate([came[s, :, g * rows : (g + 1) * rows] for s in range(n)], axis=1)
        grad[:, g * n * rows : (g + 1) * n * rows] = piece.astype(F32)
    dots[...] = jnp.sum(grad[...] * weight[...].astype(F32), axis=1, keepdims=True)


def by_line(pieces, z, n):
    for k, bit in enumerate(bits_of(n)):
        low = n >> (k + 1)
        pieces = [jnp.where((z & bit) != 0, pieces[p ^ low], pieces[p]) for p in range(n)]
    return [pieces[reversed_bits(p, n)] for p in range(n)]


def out_kernel(n, z, first, second, left, right, tap_cols):
    rows = first.shape[0] // (n // 2)
    cut = left.shape[1]
    pieces = [(first, second)[p // (n // 2)][p % (n // 2) * rows : (p % (n // 2) + 1) * rows, :] for p in range(n)]
    for p, piece in enumerate(by_line(pieces, z[0], n)):
        at = slice(p * rows, (p + 1) * rows)
        left[at, :] = piece[:, :cut]
        right[at, :] = piece[:, cut : 2 * cut]
        tap_cols[at, :] = piece[:, 2 * cut :]


def relative_kernel(n, z, term, conv_term, keep, send):
    rows = term.shape[0] // n
    width = term.shape[1]
    for value, lanes in ((term, slice(0, width)), (conv_term, slice(width, None))):
        pieces = [value[reversed_bits(p, n) * rows : (reversed_bits(p, n) + 1) * rows, :] for p in range(n)]
        for k, bit in enumerate(bits_of(n)):
            low = n >> (k + 1)
            pieces = [jnp.where((z[0] & bit) != 0, pieces[p ^ low], pieces[p]) for p in range(n)]
        for p in range(n):
            out = (keep, send)[p // (n // 2)]
            at = slice(p % (n // 2) * rows, (p % (n // 2) + 1) * rows)
            out[at, lanes] = pieces[p].astype(out.dtype)


def side_kernel(count, *refs):
    pieces, (left, right) = refs[:count], refs[count:]
    rows = pieces[0].shape[0]
    cut = left.shape[1]
    for k in range(count):
        left[k * rows : (k + 1) * rows, :] = pieces[k][:, :cut]
        right[k * rows : (k + 1) * rows, :] = pieces[k][:, cut:]


def project_kernel(channels, count, *refs):
    pieces = refs[:count]
    in_a, in_b, own_ref, normed_a, normed_b, product, c_high, c_low, b_out, x_out, own_tok = refs[count : count + 11]
    tok = refs[count + 11]
    rows = pieces[0].shape[0]
    split = in_a.shape[1]
    at_gain = 3 * channels
    gain = jnp.concatenate([in_a[at_gain : at_gain + 1, :], in_b[at_gain : at_gain + 1, :]], axis=1).astype(F32)
    for k in range(0, count, 2):
        at = slice(k * rows, (k + 2) * rows)
        for j in range(2):
            piece = pieces[k + j][...]
            here = slice((k + j) * rows, (k + j + 1) * rows)
            tok[here, :] = piece
            wide = piece.astype(F32)
            unit = wide * lax.rsqrt(jnp.mean(wide * wide, axis=1, keepdims=True) + EPS)
            lean = (unit * gain).astype(BF16)
            normed_a[here, :] = lean[:, :split]
            normed_b[here, :] = lean[:, split:]
        left, right = normed_a[at, :], normed_b[at, :]

        def part(j):
            lines = slice(j * channels, (j + 1) * channels)
            return mt(left, in_a[lines, :]) + mt(right, in_b[lines, :])

        b_part, c_part, x_part = part(0), part(1), part(2)
        high = c_part.astype(BF16)
        product[at, :] = (b_part * x_part).astype(BF16)
        c_high[at, :] = high
        c_low[at, :] = (c_part - high.astype(F32)).astype(BF16)
        b_out[at, :] = b_part
        x_out[at, :] = x_part
    lanes = lax.broadcasted_iota(jnp.int32, (own_ref.shape[0], tok.shape[0]), 1)
    own_tok[...] = mm((own_ref[...] == lanes).astype(F32).astype(BF16), tok[...]).astype(BF16)


def conv_kernel(batches, n, me, product, c_high, c_low, source, offset, taps, p_out, c_out, conv_out, gated_out, gated):
    names = gather_names(n, batches)
    group = source.shape[1]
    half = group // 2
    rows = group // n
    for m in range(batches):
        lanes = lax.broadcasted_iota(jnp.int32, (group, group), 1)
        deal = (source[m] == lanes).astype(F32).astype(BF16)
        first, second = pl.ds(m * half, half), pl.ds((batches + m) * half, half)

        def moved(ref):
            return mm(deal[:, :half], ref[first, :]) + mm(deal[:, half:], ref[second, :])

        wide = moved(product)
        c_part = moved(c_high) + moved(c_low)
        place = offset[m]
        prev_one = jnp.where(place >= 1, pltpu.roll(wide, 1, 0), 0.0)
        prev_two = jnp.where(place >= 2, pltpu.roll(wide, 2, 0), 0.0)
        conv = prev_two * taps[0:1, :] + prev_one * taps[1:2, :] + wide * taps[2:3, :]
        p_out[m] = wide.astype(BF16)
        c_out[m] = c_part
        conv_out[m] = conv
        gated[...] = c_part * conv
        for c in range(2):
            for k, e in enumerate(names[m]):
                other = me[0] ^ (2 * e + c)
                block = gated[pl.ds(pl.multiple_of(other * rows, 8), rows), :]
                at = ((c * batches + m) * (n // 2) + k) * rows
                gated_out[at : at + rows, :] = block.astype(BF16)


def summed(batches, terms):
    return jnp.concatenate([terms[m][...] + terms[batches + m][...].astype(F32) for m in range(batches)], axis=0)


def hidden_kernel(batches, n_dp, z, own_tok, gain, *refs):
    terms, (hidden, unit_out, *parts) = refs[: 2 * batches], refs[2 * batches :]
    value = exchange(own_tok[...].astype(F32), z[0], n_dp, True) + summed(batches, terms)
    hidden[...] = value
    unit = value * lax.rsqrt(jnp.mean(value * value, axis=1, keepdims=True) + EPS)
    unit_out[...] = unit
    lean = exchange(unit * gain[...], z[0], n_dp, False).astype(BF16)
    rows = parts[0].shape[0]
    for m in range(batches):
        parts[m][...] = lean[m * rows : (m + 1) * rows]


def gate_kernel(count, *refs):
    pieces = refs[:count]
    gate_a, gate_b, up_a, up_b, lean_a, lean_b, inner, by_gate, by_up = refs[count:]
    rows = pieces[0].shape[0]
    split = gate_a.shape[1]
    for k in range(0, count, 2):
        at = slice(k * rows, (k + 2) * rows)
        for j in range(2):
            here = slice((k + j) * rows, (k + j + 1) * rows)
            lean_a[here, :] = pieces[k + j][:, :split]
            lean_b[here, :] = pieces[k + j][:, split:]
        left, right = lean_a[at, :], lean_b[at, :]
        gate = mt(left, gate_a[...]) + mt(right, gate_b[...])
        up = mt(left, up_a[...]) + mt(right, up_b[...])
        sig = jax.nn.sigmoid(gate)
        silu = gate * sig
        inner[at, :] = (silu * up).astype(BF16)
        by_gate[at, :] = (up * sig * (1.0 + gate * (1.0 - sig))).astype(BF16)
        by_up[at, :] = silu.astype(BF16)


def inner_kernel(chunk, cot_a, cot_b, down_a, down_b, by_gate, by_up, d_gate, d_up):
    for k in range(cot_a.shape[0] // chunk):
        at = slice(k * chunk, (k + 1) * chunk)
        d_inner = mt(cot_a[at, :], down_a[...]) + mt(cot_b[at, :], down_b[...])
        d_gate[at, :] = (d_inner * by_gate[at, :].astype(F32)).astype(BF16)
        d_up[at, :] = (d_inner * by_up[at, :].astype(F32)).astype(BF16)


def rows_kernel(pairs, chunk, *refs):
    out = refs[-1]
    for k in range(out.shape[0] // chunk):
        at = slice(k * chunk, (k + 1) * chunk)
        for j in range(2):
            split = refs[1 + j].shape[1]
            value = mm(refs[0][at, :], refs[1 + j][...])
            for pair in range(1, pairs):
                value += mm(refs[3 * pair][at, :], refs[3 * pair + 1 + j][...])
            out[at, j * split : (j + 1) * split] = value.astype(out.dtype)


def half_rows(pairs, part, dtype, chunk):
    total = pairs[0][0].shape[0]
    width = 2 * pairs[0][1].shape[1]
    specs, arrays = [], []
    for lhs, left, right in pairs:
        specs.append(pl.BlockSpec((total // 2, lhs.shape[1]), lambda i: (part, 0)))
        specs += [pl.BlockSpec(left.shape, lambda i: (0, 0)), pl.BlockSpec(right.shape, lambda i: (0, 0))]
        arrays += [lhs, left, right]
    return pl.pallas_call(
        functools.partial(rows_kernel, len(pairs), chunk),
        out_shape=jax.ShapeDtypeStruct((total // 2, width), dtype),
        grid=(1,),
        in_specs=specs,
        out_specs=pl.BlockSpec((total // 2, width), lambda i: (0, 0)),
        compiler_params=pltpu.CompilerParams(vmem_limit_bytes=48 * 2**20),
        cost_estimate=pl.CostEstimate(flops=1000, bytes_accessed=1000, transcendentals=0),
    )(*arrays)


def branch_kernel(batches, n_dp, z, cot, hidden, unit, gain, *refs):
    terms, parts = refs[: 2 * batches], refs[2 * batches :]
    back = exchange(summed(batches, terms), z[0], n_dp, True)
    value = hidden[...]
    inv = lax.rsqrt(jnp.mean(value * value, axis=1, keepdims=True) + EPS)
    scaled = back * gain[...]
    one = unit[...]
    mean = jnp.mean(scaled * one, axis=1, keepdims=True)
    lean = (cot[...].astype(F32) + inv * (scaled - one * mean)).astype(BF16)
    rows = parts[0].shape[0]
    for m in range(batches):
        parts[m][...] = lean[m * rows : (m + 1) * rows]


def conv_back_kernel(batches, n, count, me, *refs):
    pieces = refs[:count]
    out_a, out_b, conv, c_nat, p_nat, b_arr, x_arr, source, offset, slot, taps = refs[count : count + 11]
    branch, d_b, d_c, d_x, conv_grad, own, natural = refs[count + 11 :]
    total = branch.shape[0]
    group = total // batches
    half = group // 2
    rows = group // n
    cut = out_a.shape[1]
    names = gather_names(n, batches)
    for k in range(count):
        size = pieces[k].shape[0]
        branch[k * size : (k + 1) * size, :] = pieces[k][...]
    for c in range(2):
        for m in range(batches):
            k = c * batches + m
            at = slice(k * half, (k + 1) * half)
            gated = mt(branch[at, :cut], out_a[...]) + mt(branch[at, cut:], out_b[...])
            for j, e in enumerate(names[m]):
                other = me[0] ^ (2 * e + c)
                at = m * group + other * rows
                natural[pl.ds(pl.multiple_of(at, 8), rows), :] = gated[j * rows : (j + 1) * rows]
    totals = [jnp.zeros((1, taps.shape[1]), F32)] * 3
    for m in range(batches):
        gated = natural[m * group : (m + 1) * group, :]
        place = offset[m]
        wide = p_nat[m].astype(F32)
        grad = gated * c_nat[m]
        grad_c = (gated * conv[m]).astype(BF16)
        one = jnp.where(place >= 1, grad, 0.0)
        two = jnp.where(place >= 2, grad, 0.0)
        totals[0] += jnp.sum(two * pltpu.roll(wide, 2, 0), axis=0, keepdims=True)
        totals[1] += jnp.sum(one * pltpu.roll(wide, 1, 0), axis=0, keepdims=True)
        totals[2] += jnp.sum(grad * wide, axis=0, keepdims=True)
        d_product = (
            grad * taps[2:3, :]
            + pltpu.roll(one, group - 1, 0) * taps[1:2, :]
            + pltpu.roll(two, group - 2, 0) * taps[0:1, :]
        ).astype(BF16)
        lines = lax.broadcasted_iota(jnp.int32, (group, group), 0)
        undeal = (source[m] == lines).astype(F32).astype(BF16)
        d_prod = mm(undeal, d_product)
        c_back = mm(undeal, grad_c)
        for c in range(2):
            there = pl.ds((c * batches + m) * half, half)
            piece = d_prod[c * half : (c + 1) * half]
            d_b[there, :] = (piece * x_arr[there, :]).astype(BF16)
            d_c[there, :] = c_back[c * half : (c + 1) * half].astype(BF16)
            d_x[there, :] = (piece * b_arr[there, :]).astype(BF16)
    for k in range(3):
        conv_grad[k : k + 1, :] = totals[k]
    lanes = lax.broadcasted_iota(jnp.int32, (slot.shape[0], total), 1)
    picked = (slot[...] == lanes).astype(F32).astype(BF16)
    own[...] = mm(picked, branch[...]).astype(BF16)


def final_kernel(batches, n_dp, z, tokens, gain, d_hidden, *refs):
    terms, out = refs[:-1], refs[-1]
    back = exchange(summed(batches, terms), z[0], n_dp, True)
    wide = tokens[...].astype(F32)
    inv = lax.rsqrt(jnp.mean(wide * wide, axis=1, keepdims=True) + EPS)
    unit = wide * inv
    scaled = back * gain[...]
    mean = jnp.mean(scaled * unit, axis=1, keepdims=True)
    out[...] = (d_hidden[...].astype(F32) + inv * (scaled - unit * mean)).astype(BF16)


def block_kernel(batches, n_dp, z, hidden, *refs):
    terms, out = refs[:-1], refs[-1]
    out[...] = (hidden[...] + exchange(summed(batches, terms), z[0], n_dp, True)).astype(BF16)


def body(
    tokens_in,
    in_weight,
    conv_weight,
    out_weight,
    norm_gain,
    ff_gain,
    gate_weight,
    up_weight,
    down_weight,
    cotangent,
    deal_table,
    seq_lengths,
):
    batches, rows_dev, width = tokens_in.shape
    n, n_dp = lax.axis_size("shard"), lax.axis_size("dp")
    half = n // 2
    me, z = lax.axis_index("shard"), lax.axis_index("dp")
    group = n * rows_dev
    piece_rows = rows_dev // n
    own_rows, hidden_units = gate_weight.shape
    total = batches * group
    outer = bits_of(n)[1:]
    zblock = n * own_rows
    channels = n_dp * own_rows

    whole = hidden_units // (LANES * n) * LANES
    rest = hidden_units // n - whole

    place = jnp.arange(zblock, dtype=jnp.int32)
    identity = (place[:, None] == place[None, :]).astype(BF16)
    own_total = batches * rows_dev
    share = hidden_units // n
    chunk = total // 4
    cut = width // 2
    names = gather_names(n, batches)

    def dealt(blocks):
        return lax.all_to_all(blocks, "shard", split_axis=0, concat_axis=0, tiled=True)

    def flipped(block):
        return dot(block.reshape(zblock, -1), identity, ((0,), (0,)), BF16)

    in_parts = in_weight.reshape(own_rows, 3 * n_dp, n, own_rows).transpose(2, 0, 1, 3)
    in_parts = in_parts.reshape(n, own_rows, 3 * channels)
    spare = 14
    table = deal_table[:, 0, 0, :].astype(BF16).reshape(-1)
    table = jnp.pad(table, (0, own_rows * spare - table.shape[0])).reshape(own_rows, spare)
    extra = jnp.concatenate([norm_gain[:, None], ff_gain[:, None], table], axis=1)
    in_parts = jnp.concatenate([in_parts, jnp.broadcast_to(extra[None], (n,) + extra.shape)], axis=2)
    in_came = dealt(in_parts)
    tok_turned = turned(tokens_in, z, n_dp)
    tok_pieces, tok_steps = plane_gather([tok_turned[m] for m in range(batches)])
    out_aug = jnp.concatenate(
        [out_weight, conv_weight, jnp.zeros((own_rows, LANES - conv_weight.shape[1]), BF16)], axis=1
    )
    out_lines = out_aug
    for bit in reversed(bits_of(n_dp)):
        out_came = swap(out_lines, bit, "dp")
        if bit > 1:
            out_lines = jnp.concatenate([out_lines, out_came], axis=0)

    in_a, in_b, ready = line_gather(flipped(in_came))
    weights = [gate_weight, up_weight, down_weight]
    [ff_parts] = run(
        functools.partial(spread_kernel, n, whole, rest, 3),
        [((n, 3 * own_rows, share), BF16)],
        [],
        weights,
    )
    ff_came = dealt(after(ff_parts, in_came))
    gate_block, up_block, down_block = [
        flipped(ff_came[:, k * own_rows : (k + 1) * own_rows]) for k in range(3)
    ]
    gate_a, gate_b, ready = line_gather(gate_block, ready)
    gate_high = ready
    up_a, up_b, ready = line_gather(up_block, ready)
    up_high = ready
    down_a, down_b, ready = line_gather(down_block, ready)
    down_high = ready

    def natural_row(row):
        both = jnp.concatenate([in_a[row : row + 1], in_b[row : row + 1]], axis=1)
        step = width // n_dp
        out = None
        for k in range(n_dp):
            order = [reversed_bits(k ^ p, n_dp) for p in range(n_dp)]
            moved = jnp.concatenate([both[:, q * step : (q + 1) * step] for q in order], axis=1)
            out = moved if out is None else jnp.where(z == k, moved, out)
        return out.astype(F32)

    gain_one = natural_row(3 * channels)
    gain_two = natural_row(3 * channels + 1)
    out_a, out_b, tap_cols = run(
        functools.partial(out_kernel, n_dp),
        [((channels, cut), BF16), ((channels, cut), BF16), ((channels, LANES), BF16)],
        [z],
        [out_lines, out_came],
    )
    taps = tap_cols[:, : conv_weight.shape[1]].astype(F32).T

    deal = in_came[:, :, 3 * channels + 2 :].reshape(n, own_rows * spare)[:, : batches * n]
    deal = deal.reshape(n, batches, n).transpose(1, 0, 2).astype(jnp.int32)
    m_index = jnp.arange(batches, dtype=jnp.int32)[:, None, None, None]
    j_index = jnp.arange(n, dtype=jnp.int32)[None, :, None, None]
    t_index = jnp.arange(piece_rows, dtype=jnp.int32)[None, None, None, :]

    def place_of(e, m):
        out = jnp.zeros_like(e + m)
        for part in range(batches):
            for k, name in enumerate(names[part]):
                out = jnp.where((e == name) & (m == part), k, out)
        return out

    def within(m, holder, row):
        rel = holder ^ me
        return ((rel & 1) * half + place_of(rel >> 1, m)) * rows_dev + row

    def arrival_row(m, holder, row):
        rel = holder ^ me
        return (((rel & 1) * batches + m) * half + place_of(rel >> 1, m)) * rows_dev + row

    slot_row = j_index * piece_rows + t_index
    source = within(m_index, deal[:, :, :, None], slot_row).reshape(batches, group)
    own_deal = lax.dynamic_index_in_dim(deal, me, 1, keepdims=True)[:, :, :, None]
    own_source = arrival_row(m_index, own_deal, me * piece_rows + t_index).reshape(own_total, 1)
    inverse = jnp.sum(jnp.where(deal == me, jnp.arange(n, dtype=jnp.int32)[None, None, :], 0), axis=2)
    slot_source = arrival_row(
        m_index[:, :, 0], j_index[:, :, 0], inverse[:, :, None] * piece_rows + t_index[:, 0]
    ).reshape(own_total, 1)

    lengths = seq_lengths[:, 0, :]
    places = jnp.arange(group, dtype=jnp.int32)
    seq_start = jnp.zeros((batches, group), jnp.int32)
    start = jnp.zeros((batches,), jnp.int32)
    for k in range(lengths.shape[1]):
        seq_start = jnp.where(start[:, None] <= places[None, :], start[:, None], seq_start)
        start = start + lengths[:, k]
    offset = (places[None, :] - seq_start)[:, :, None]

    arr = (total, channels)
    nat = (batches, group, channels)
    own = (own_total, width)
    side = (total, cut)
    normed_a, normed_b, product, c_high, c_low, b_arr, x_arr, own_tok = run(
        functools.partial(project_kernel, channels, len(tok_pieces)),
        [(side, BF16), (side, BF16), (arr, BF16), (arr, BF16), (arr, BF16), (arr, F32), (arr, F32), (own, BF16)],
        [],
        [*tok_pieces, in_a, in_b, own_source],
        [pltpu.VMEM((total, width), BF16)],
    )
    p_nat, c_nat, conv_out, gated_arr = run(
        functools.partial(conv_kernel, batches, n),
        [(nat, BF16), (nat, F32), (nat, F32), (arr, BF16)],
        [me],
        [product, c_high, c_low, source[:, :, None], offset, taps],
        [pltpu.VMEM((group, channels), F32)],
    )
    cot_turned = turned(cotangent, z, n_dp)
    cot_pieces, cot_steps = plane_gather([cot_turned[m] for m in range(batches)], ((ff_came, *tok_steps[-1]), ()))

    def summed_rows(*pairs, wait=()):
        far = half_rows(pairs, 1, BF16, chunk)
        near = half_rows(pairs, 0, F32, chunk)
        return plane_reduce(near, far, batches, wait)

    mine = ((rows_dev, width), BF16)
    hidden, unit_two, *ff_own = run(
        functools.partial(hidden_kernel, batches, n_dp),
        [(own, F32), (own, F32)] + [mine] * batches,
        [z],
        [own_tok, gain_two, *summed_rows((gated_arr, out_a, out_b), wait=(*gate_high, *cot_steps[-1]))],
    )
    ff_pieces, ff_steps = plane_gather(ff_own, ((), (gate_b, *up_high)))
    cot_a, cot_b = run(
        functools.partial(side_kernel, len(cot_pieces)), [(side, BF16), (side, BF16)], [], cot_pieces
    )

    ff = (total, share)
    ff_pieces[0] = after(ff_pieces[0], *down_high)
    lean_a, lean_b, ff_inner, by_gate, by_up = run(
        functools.partial(gate_kernel, len(ff_pieces)),
        [(side, BF16), (side, BF16), (ff, BF16), (ff, BF16), (ff, BF16)],
        [],
        [*ff_pieces, gate_a, gate_b, up_a, up_b],
    )

    def outer_sum(former, left, right, wait=None):
        send = dot(former, right, ((0,), (0,)), BF16)
        keep = dot(former, left, ((0,), (0,)))
        return line_reduce(keep, send, wait)

    def returned(terms, *wait):
        value = (terms[0] + terms[1].astype(F32)).astype(BF16)
        rows = dot(identity, value, ((1,), (1,)), BF16)
        return dealt(after(rows.reshape(n, own_rows, -1), *wait))

    *down_sum, down_low = outer_sum(ff_inner, cot_a, cot_b)
    d_gate, d_up = run(
        functools.partial(inner_kernel, chunk),
        [(ff, BF16), (ff, BF16)],
        [],
        [cot_a, cot_b, down_a, down_b, by_gate, by_up],
    )
    d_ff = summed_rows((d_gate, gate_a, gate_b), (d_up, up_a, up_b), wait=down_low)
    *gate_sum, gate_low = outer_sum(d_gate, lean_a, lean_b, down_low)
    *up_sum, up_low = outer_sum(d_up, lean_a, lean_b, gate_low)
    cot_own = cotangent.reshape(own)
    branch_own = run(
        functools.partial(branch_kernel, batches, n_dp),
        [mine] * batches,
        [z],
        [cot_own, hidden, unit_two, gain_two, *d_ff],
    )
    branch_pieces, branch_steps = plane_gather(branch_own, (gate_low, ()))
    block_sum = summed_rows((ff_inner, down_a, down_b), wait=branch_steps[-1])
    [block_out] = run(functools.partial(block_kernel, batches, n_dp), [(own, BF16)], [z], [hidden, *block_sum])
    block_out = block_out.reshape(tokens_in.shape)
    down_back = returned(down_sum, *branch_steps[-1])

    branch_pieces[0] = after(branch_pieces[0], *up_low)
    branch, *d_proj, conv_term, d_hidden_own = run(
        functools.partial(conv_back_kernel, batches, n, len(branch_pieces)),
        [((total, width), BF16), (arr, BF16), (arr, BF16), (arr, BF16), ((3, channels), F32), (own, BF16)],
        [me],
        [
            *branch_pieces,
            out_a,
            out_b,
            conv_out,
            c_nat,
            p_nat,
            b_arr,
            x_arr,
            source[:, None, :],
            offset,
            slot_source,
            taps,
        ],
        [pltpu.VMEM((total, channels), F32)],
    )
    rows_of = [slice(k * channels, (k + 1) * channels) for k in range(3)]
    gate_back = returned(gate_sum, down_back)
    d_normed = summed_rows(
        *[(d_proj[k], in_a[rows_of[k]], in_b[rows_of[k]]) for k in range(3)], wait=(down_back, gate_back)
    )
    [tokens_grad] = run(
        functools.partial(final_kernel, batches, n_dp),
        [(own, BF16)],
        [z],
        [tokens_in.reshape(own), gain_one, d_hidden_own, *d_normed],
    )
    tokens_grad = tokens_grad.reshape(tokens_in.shape)

    in_send = jnp.concatenate([dot(d_proj[k], normed_b, ((0,), (0,)), BF16) for k in range(3)], axis=0)
    in_keep = jnp.concatenate([dot(d_proj[k], normed_a, ((0,), (0,))) for k in range(3)], axis=0)
    *in_sum, in_low = line_reduce(in_keep, in_send, up_low)
    up_back = returned(up_sum)
    conv_cols = jnp.pad(conv_term.T, ((0, 0), (0, LANES - conv_term.shape[0])))
    keep, send = run(
        functools.partial(relative_kernel, n_dp),
        [((channels // 2, width + LANES), F32), ((channels // 2, width + LANES), BF16)],
        [z],
        [dot(gated_arr, branch, ((0,), (0,))), conv_cols],
    )
    send = after(send, *in_low)
    for bit in bits_of(n_dp):
        came = swap(send, bit, "dp").astype(F32)
        keep = keep + came
        if 2 * bit < n_dp:
            keep, send = jnp.split(keep, 2, axis=0)
            send = send.astype(BF16)
    out_grad = keep[:, :width]
    conv_grad = keep[:, width : width + conv_weight.shape[1]]
    in_back = returned(in_sum)

    def joined(kernel, came, weight):
        shape = weight.shape
        return run(kernel, [(shape, F32), ((own_rows, 1), F32)], [], [came, weight])

    join = functools.partial(join_kernel, n, whole, rest)
    down_grad, _ = joined(join, down_back, down_weight)
    gate_grad, gate_dots = joined(join, gate_back, gate_weight)
    up_grad, up_dots = joined(join, up_back, up_weight)
    in_grad, in_dots = joined(functools.partial(join_in_kernel, n, 3 * n_dp), in_back, in_weight)
    norm_gain_grad = in_dots[:, 0] / norm_gain.astype(F32)
    ff_gain_grad = (gate_dots + up_dots)[:, 0] / ff_gain.astype(F32)
    return (
        block_out,
        tokens_grad,
        in_grad,
        conv_grad,
        out_grad,
        norm_gain_grad,
        ff_gain_grad,
        gate_grad,
        up_grad,
        down_grad,
    )


def solution(mesh):
    rows = P(("dp", "shard"), None)
    tokens = P(None, ("dp", "shard"), None)
    vector = P(("dp", "shard"))
    placed = (
        tokens,
        rows,
        rows,
        rows,
        vector,
        vector,
        rows,
        rows,
        rows,
        tokens,
        P(None, "dp", "shard", None),
        P(None, "dp", None),
    )
    return jax.shard_map(
        body,
        mesh=mesh,
        in_specs=placed,
        out_specs=(tokens, tokens, rows, rows, rows, vector, vector, rows, rows, rows),
        check_vma=False,
    )
```

```python
import functools

import jax
import jax.numpy as jnp
from jax import lax
from jax.experimental import pallas as pl
from jax.experimental.pallas import tpu as pltpu
from jax.sharding import PartitionSpec as P

EPS = 1e-05
F32 = jnp.float32
BF16 = jnp.bfloat16
LANES = 128


def dot(former, latter, dims, out=F32):
    return lax.dot_general(
        former, latter, ((dims[0], dims[1]), ((), ())), preferred_element_type=F32
    ).astype(out)


def bits_of(count):
    return [1 << k for k in range(count.bit_length() - 1)]


def swap(value, bit, axis="shard"):
    n = lax.axis_size(axis)
    return lax.ppermute(value, axis, [(i, i ^ bit) for i in range(n)])


def route(outer, turn):
    turn = turn % len(outer)
    return outer[turn:] + outer[:turn]


def after(value, *others):
    others = [other for other in others if other is not None]
    if not others:
        return value
    return lax.optimization_barrier((value, *others))[0]


def gather_names(n, parts):
    outer = bits_of(n)[1:]
    names = []
    for m in range(parts):
        order = [0]
        for bit in route(outer, m):
            order = order + [e ^ (bit >> 1) for e in order]
        names.append(order)
    return names


def plane_gather(parts, waits=((), ())):
    n = lax.axis_size("shard")
    outer = bits_of(n)[1:]
    held = [[part] for part in parts]
    steps = []
    for k in range(len(outer)):
        going = [h[0] if len(h) == 1 else jnp.concatenate(h, axis=0) for h in held]
        if k < len(waits):
            going = [after(g, *waits[k]) for g in going]
        came = [swap(going[m], route(outer, m)[k]) for m in range(len(parts))]
        held = [[g, c] for g, c in zip(going, came)]
        steps.append(tuple(came))
    near = [piece for h in held for piece in h]
    far = [swap(piece, 1) for piece in near]
    return near + far, steps


def fold_kernel(rows, plans, *refs):
    count = len(plans)
    kept, came, sends, keeps = (refs[k * count : (k + 1) * count] for k in range(4))
    for m, (going, staying) in enumerate(plans):
        for out, places in ((sends[m], going), (keeps[m], staying)):
            for k, place in enumerate(places):
                at = slice(place * rows, (place + 1) * rows)
                value = kept[m][at, :] + came[m][at, :].astype(F32)
                out[k * rows : (k + 1) * rows, :] = value.astype(out.dtype)


def first_fold_kernel(rows, plans, near, *refs):
    count = len(plans)
    came, sends, keeps = refs[: len(refs) - 2 * count], refs[len(refs) - 2 * count : -count], refs[-count:]
    per = came[0].shape[0] // rows
    for m, (going, staying) in enumerate(plans):
        for out, places in ((sends[m], going), (keeps[m], staying)):
            for k, place in enumerate(places):
                at = slice(place * rows, (place + 1) * rows)
                there = slice(place % per * rows, (place % per + 1) * rows)
                value = near[at, :] + came[place // per][there, :].astype(F32)
                out[k * rows : (k + 1) * rows, :] = value.astype(out.dtype)


def plane_reduce(near, came, parts, wait=()):
    n = lax.axis_size("shard")
    half = n // 2
    outer = bits_of(n)[1:]
    width = near.shape[1]
    rows = near.shape[0] // (parts * half)
    names = gather_names(n, parts)
    kept, arrived = near, came
    for k in reversed(range(len(outer))):
        plans = []
        for m in range(parts):
            bit = route(outer, m)[k] >> 1
            going = [e for e in names[m] if e & bit]
            base = m * half if kept is near else 0
            plans.append(([base + names[m].index(e) for e in going], [base + names[m].index(e ^ bit) for e in going]))
            names[m] = [e ^ bit for e in going]
        shape = (len(plans[0][0]) * rows, width)
        outs = [(shape, BF16)] * parts + [(shape, F32)] * parts
        if kept is near:
            made = run(functools.partial(first_fold_kernel, rows, plans), outs, [], [near, *came])
            sends = [after(send, *wait) for send in made[:parts]]
        else:
            made = run(functools.partial(fold_kernel, rows, plans), outs, [], [*kept, *arrived])
            sends = made[:parts]
        first = kept is near
        kept = made[parts:]
        arrived = [swap(sends[m], route(outer, m)[k]) for m in range(parts)]
        if first:
            first_came = arrived
    return [*kept, *arrived], first_came


def line_gather(block, waits=((), ())):
    n = lax.axis_size("dp")
    block = after(block, *waits[0])
    for bit in reversed(bits_of(n)):
        came = swap(block, bit, "dp")
        if bit == 1:
            return block, came
        block = after(jnp.concatenate([block, came], axis=1), *waits[1])


def line_reduce(keep, send, wait=()):
    n = lax.axis_size("dp")
    for bit in bits_of(n):
        came = swap(send, bit, "dp")
        if 2 * bit == n:
            return keep, came
        total = keep + came.astype(F32)
        cut = total.shape[0] // 2
        keep, send = total[:cut], after(total[cut:].astype(BF16), *wait)


def reversed_bits(index, n):
    out = 0
    for k, bit in enumerate(bits_of(n)):
        if index & bit:
            out |= n >> (k + 1)
    return out


def turned(value, z, n):
    step = value.shape[-1] // n
    pieces = [value[..., k * step : (k + 1) * step] for k in range(n)]
    out = None
    for k in range(n):
        order = [pieces[k ^ reversed_bits(p, n)] for p in range(n)]
        moved = jnp.concatenate(order, axis=-1)
        out = moved if out is None else jnp.where(z == k, moved, out)
    return out


def exchange(value, z, n, back):
    step = value.shape[1] // n
    pieces = [value[:, p * step : (p + 1) * step] for p in range(n)]

    def reorder(pieces):
        return [pieces[reversed_bits(p, n)] for p in range(n)]

    def flip(pieces):
        for k, bit in enumerate(bits_of(n)):
            low = n >> (k + 1)
            pieces = [jnp.where((z & bit) != 0, pieces[p ^ low], pieces[p]) for p in range(n)]
        return pieces

    return jnp.concatenate(reorder(flip(pieces)) if back else flip(reorder(pieces)), axis=1)


WHOLE = pl.BlockSpec(memory_space=pltpu.VMEM)
SCALAR = pl.BlockSpec(memory_space=pltpu.SMEM)


def run(kernel, outs, scalars, arrays, scratch=()):
    return pl.pallas_call(
        kernel,
        out_shape=[jax.ShapeDtypeStruct(shape, dtype) for shape, dtype in outs],
        in_specs=[SCALAR] * len(scalars) + [WHOLE] * len(arrays),
        out_specs=[WHOLE] * len(outs),
        scratch_shapes=list(scratch),
        compiler_params=pltpu.CompilerParams(vmem_limit_bytes=48 * 2**20),
        cost_estimate=pl.CostEstimate(flops=1000, bytes_accessed=1000, transcendentals=0),
    )(*[jnp.asarray(v, jnp.int32).reshape(1) for v in scalars], *arrays)


def mm(former, latter):
    return lax.dot_general(former, latter, (((1,), (0,)), ((), ())), preferred_element_type=F32)


def mt(former, latter):
    return lax.dot_general(former, latter, (((1,), (1,)), ((), ())), preferred_element_type=F32)


def spread_kernel(n, whole, rest, count, *refs):
    weights, out = refs[:count], refs[count]
    rows = weights[0].shape[0]
    for k in range(count):
        for s in range(n):
            at = slice(k * rows, (k + 1) * rows)
            first = n * whole + s * rest
            out[s, at, :whole] = weights[k][:, s * whole : (s + 1) * whole]
            out[s, at, whole:] = weights[k][:, first : first + rest]


def join_kernel(n, whole, rest, count, came, *refs):
    weights, outs = refs[:count], refs[count:]
    share = whole + rest
    for k in range(count):
        grad, dots = outs[2 * k : 2 * k + 2]
        first = k * share
        tails = [came[s, :, first + whole : first + share] for s in range(n)]
        grad[:, n * whole :] = jnp.concatenate(tails, axis=1).astype(F32)
        for s in range(n):
            grad[:, s * whole : (s + 1) * whole] = came[s, :, first : first + whole].astype(F32)
        dots[...] = jnp.sum(grad[...] * weights[k][...].astype(F32), axis=1, keepdims=True)


def join_in_kernel(n, groups, came, weight, grad, dots):
    rows = came.shape[1]
    for g in range(groups):
        piece = jnp.concatenate([came[s, :, g * rows : (g + 1) * rows] for s in range(n)], axis=1)
        grad[:, g * n * rows : (g + 1) * n * rows] = piece.astype(F32)
    dots[...] = jnp.sum(grad[...] * weight[...].astype(F32), axis=1, keepdims=True)


def by_line(pieces, z, n):
    for k, bit in enumerate(bits_of(n)):
        low = n >> (k + 1)
        pieces = [jnp.where((z & bit) != 0, pieces[p ^ low], pieces[p]) for p in range(n)]
    return [pieces[reversed_bits(p, n)] for p in range(n)]


def out_kernel(n, z, first, second, full, tap_cols):
    rows = first.shape[0] // (n // 2)
    width = full.shape[1]
    pieces = [(first, second)[p // (n // 2)][p % (n // 2) * rows : (p % (n // 2) + 1) * rows, :] for p in range(n)]
    for p, piece in enumerate(by_line(pieces, z[0], n)):
        at = slice(p * rows, (p + 1) * rows)
        full[at, :] = piece[:, :width]
        tap_cols[at, :] = piece[:, width:]


def relative_kernel(n, z, term, conv_term, keep, send):
    rows = term.shape[0] // n
    width = term.shape[1]
    for value, lanes in ((term, slice(0, width)), (conv_term, slice(width, None))):
        pieces = [value[reversed_bits(p, n) * rows : (reversed_bits(p, n) + 1) * rows, :] for p in range(n)]
        for k, bit in enumerate(bits_of(n)):
            low = n >> (k + 1)
            pieces = [jnp.where((z[0] & bit) != 0, pieces[p ^ low], pieces[p]) for p in range(n)]
        for p in range(n):
            out = (keep, send)[p // (n // 2)]
            at = slice(p % (n // 2) * rows, (p % (n // 2) + 1) * rows)
            out[at, lanes] = pieces[p].astype(out.dtype)


def stack_kernel(count, *refs):
    pieces, out = refs[:count], refs[count]
    rows = pieces[0].shape[0]
    for k in range(count):
        out[k * rows : (k + 1) * rows, :] = pieces[k][...]


def product_kernel(former, latter, out):
    out[...] = mm(former[...], latter[...]).astype(out.dtype)


def product(former, latter, blocks):
    rows = former.shape[0] // blocks
    return pl.pallas_call(
        product_kernel,
        out_shape=jax.ShapeDtypeStruct((former.shape[0], latter.shape[1]), BF16),
        grid=(blocks,),
        in_specs=[
            pl.BlockSpec((rows, former.shape[1]), lambda i: (i, 0)),
            pl.BlockSpec(latter.shape, lambda i: (0, 0)),
        ],
        out_specs=pl.BlockSpec((rows, latter.shape[1]), lambda i: (i, 0)),
        compiler_params=pltpu.CompilerParams(vmem_limit_bytes=48 * 2**20),
        cost_estimate=pl.CostEstimate(flops=1000, bytes_accessed=1000, transcendentals=0),
    )(former, latter)


def columns_kernel(chunk, rows, out):
    for k in range(rows.shape[1] // chunk):
        at = slice(k * chunk, (k + 1) * chunk)
        out[at, :] = rows[:, at].astype(F32).T.astype(BF16)


def project_kernel(channels, count, *refs):
    pieces = refs[:count]
    in_a, in_b, own_ref, normed_a, normed_b, product, c_high, c_low, b_out, x_out, own_tok = refs[count : count + 11]
    tok = refs[count + 11]
    rows = pieces[0].shape[0]
    split = in_a.shape[1]
    at_gain = 3 * channels
    gain = jnp.concatenate([in_a[at_gain : at_gain + 1, :], in_b[at_gain : at_gain + 1, :]], axis=1).astype(F32)
    for k in range(0, count, 2):
        at = slice(k * rows, (k + 2) * rows)
        for j in range(2):
            piece = pieces[k + j][...]
            here = slice((k + j) * rows, (k + j + 1) * rows)
            tok[here, :] = piece
            wide = piece.astype(F32)
            unit = wide * lax.rsqrt(jnp.mean(wide * wide, axis=1, keepdims=True) + EPS)
            lean = (unit * gain).astype(BF16)
            normed_a[here, :] = lean[:, :split]
            normed_b[here, :] = lean[:, split:]
        left, right = normed_a[at, :], normed_b[at, :]

        def part(j):
            lines = slice(j * channels, (j + 1) * channels)
            return mt(left, in_a[lines, :]) + mt(right, in_b[lines, :])

        b_part, c_part, x_part = part(0), part(1), part(2)
        high = c_part.astype(BF16)
        product[at, :] = (b_part * x_part).astype(BF16)
        c_high[at, :] = high
        c_low[at, :] = (c_part - high.astype(F32)).astype(BF16)
        b_out[at, :] = b_part
        x_out[at, :] = x_part
    lanes = lax.broadcasted_iota(jnp.int32, (own_ref.shape[0], tok.shape[0]), 1)
    own_tok[...] = mm((own_ref[...] == lanes).astype(F32).astype(BF16), tok[...]).astype(BF16)


def conv_kernel(batches, n, me, product, c_high, c_low, source, offset, taps, p_out, c_out, conv_out, gated_out, gated):
    names = gather_names(n, batches)
    group = source.shape[1]
    half = group // 2
    rows = group // n
    for m in range(batches):
        lanes = lax.broadcasted_iota(jnp.int32, (group, group), 1)
        deal = (source[m] == lanes).astype(F32).astype(BF16)
        first, second = pl.ds(m * half, half), pl.ds((batches + m) * half, half)

        def moved(ref):
            return mm(deal[:, :half], ref[first, :]) + mm(deal[:, half:], ref[second, :])

        wide = moved(product)
        c_part = moved(c_high) + moved(c_low)
        place = offset[m]
        prev_one = jnp.where(place >= 1, pltpu.roll(wide, 1, 0), 0.0)
        prev_two = jnp.where(place >= 2, pltpu.roll(wide, 2, 0), 0.0)
        conv = prev_two * taps[0:1, :] + prev_one * taps[1:2, :] + wide * taps[2:3, :]
        p_out[m] = wide.astype(BF16)
        c_out[m] = c_part
        conv_out[m] = conv
        gated[...] = c_part * conv
        for c in range(2):
            for k, e in enumerate(names[m]):
                other = me[0] ^ (2 * e + c)
                block = gated[pl.ds(pl.multiple_of(other * rows, 8), rows), :]
                at = ((c * batches + m) * (n // 2) + k) * rows
                gated_out[at : at + rows, :] = block.astype(BF16)


def summed(batches, terms):
    return jnp.concatenate([terms[m][...] + terms[batches + m][...].astype(F32) for m in range(batches)], axis=0)


def hidden_kernel(batches, n_dp, z, own_tok, gain, *refs):
    terms, (hidden, unit_out, *parts) = refs[: 2 * batches], refs[2 * batches :]
    value = exchange(own_tok[...].astype(F32), z[0], n_dp, True) + summed(batches, terms)
    hidden[...] = value
    unit = value * lax.rsqrt(jnp.mean(value * value, axis=1, keepdims=True) + EPS)
    unit_out[...] = unit
    lean = (unit * gain[...]).astype(BF16)
    rows = parts[0].shape[0]
    for m in range(batches):
        parts[m][...] = lean[m * rows : (m + 1) * rows]


def gate_kernel(count, *refs):
    pieces = refs[:count]
    two, lean, inner, by_gate, by_up = refs[count:]
    rows = pieces[0].shape[0]
    share = two.shape[0] // 2
    for k in range(0, count, 2):
        at = slice(k * rows, (k + 2) * rows)
        for j in range(2):
            lean[(k + j) * rows : (k + j + 1) * rows, :] = pieces[k + j][...]
        part = lean[at, :]
        gate = mt(part, two[:share, :])
        up = mt(part, two[share:, :])
        sig = jax.nn.sigmoid(gate)
        silu = gate * sig
        inner[at, :] = (silu * up).astype(BF16)
        by_gate[at, :] = (up * sig * (1.0 + gate * (1.0 - sig))).astype(BF16)
        by_up[at, :] = silu.astype(BF16)


def inner_kernel(chunk, cot, down, by_gate, by_up, *refs):
    d_two = refs[-1]
    share = by_gate.shape[1]
    for k in range(cot.shape[0] // chunk):
        at = slice(k * chunk, (k + 1) * chunk)
        d_inner = mt(cot[at, :], down[...])
        d_two[at, :share] = (d_inner * by_gate[at, :].astype(F32)).astype(BF16)
        d_two[at, share:] = (d_inner * by_up[at, :].astype(F32)).astype(BF16)


def inner_half(part, chunk, cot, down, by_gate, by_up, other=None):
    total, share = by_gate.shape

    def rows_of(width):
        return pl.BlockSpec((total // 2, width), lambda i: (part, 0))

    extra = [] if other is None else [other]
    return pl.pallas_call(
        functools.partial(inner_kernel, chunk),
        out_shape=jax.ShapeDtypeStruct((total, 2 * share), BF16),
        grid=(1,),
        in_specs=[rows_of(cot.shape[1]), pl.BlockSpec(down.shape, lambda i: (0, 0)), rows_of(share), rows_of(share)]
        + [pl.BlockSpec(memory_space=pl.ANY)] * len(extra),
        out_specs=rows_of(2 * share),
        input_output_aliases={4: 0} if extra else {},
        compiler_params=pltpu.CompilerParams(vmem_limit_bytes=48 * 2**20),
        cost_estimate=pl.CostEstimate(flops=1000, bytes_accessed=1000, transcendentals=0),
    )(cot, down, by_gate, by_up, *extra)


def rows_kernel(*refs, sides):
    lhs, rhs, outs = refs[0], refs[1 : 1 + sides], refs[1 + sides :]
    rows = outs[0].shape[0]
    per = max(1, 384 // rows)
    step = min(rows, 384)
    for k in range(0, len(outs), per):
        count = min(per, len(outs) - k)
        for first in range(0, rows, step):
            at = slice(k * rows + first, k * rows + first + step * count)
            for j in range(sides):
                split = rhs[j].shape[1]
                value = mm(lhs[at, :], rhs[j][...])
                for piece in range(count):
                    here = value[piece * step : (piece + 1) * step]
                    outs[k + piece][first : first + step, j * split : (j + 1) * split] = here.astype(outs[0].dtype)


def half_rows(lhs, rhs, part, dtype, pieces):
    rows = lhs.shape[0] // 2
    width = sum(side.shape[1] for side in rhs)
    shape = (rows // pieces, width)
    return pl.pallas_call(
        functools.partial(rows_kernel, sides=len(rhs)),
        out_shape=[jax.ShapeDtypeStruct(shape, dtype)] * pieces,
        grid=(1,),
        in_specs=[pl.BlockSpec((rows, lhs.shape[1]), lambda i: (part, 0))]
        + [pl.BlockSpec(side.shape, lambda i: (0, 0)) for side in rhs],
        out_specs=[pl.BlockSpec(shape, lambda i: (0, 0))] * pieces,
        compiler_params=pltpu.CompilerParams(vmem_limit_bytes=48 * 2**20),
        cost_estimate=pl.CostEstimate(flops=1000, bytes_accessed=1000, transcendentals=0),
    )(lhs, *rhs)


def branch_kernel(batches, cot, hidden, unit, gain, *refs):
    terms, parts = refs[: 2 * batches], refs[2 * batches :]
    value = hidden[...]
    inv = lax.rsqrt(jnp.mean(value * value, axis=1, keepdims=True) + EPS)
    scaled = summed(batches, terms) * gain[...]
    one = unit[...]
    mean = jnp.mean(scaled * one, axis=1, keepdims=True)
    lean = (cot[...].astype(F32) + inv * (scaled - one * mean)).astype(BF16)
    rows = parts[0].shape[0]
    for m in range(batches):
        parts[m][...] = lean[m * rows : (m + 1) * rows]


def conv_back_kernel(batches, n, count, me, *refs):
    pieces = refs[:count]
    out_ref, conv, c_nat, p_nat, b_arr, x_arr, source, offset, slot, taps = refs[count : count + 10]
    branch, d_proj, conv_grad, own, natural = refs[count + 10 :]
    channels = taps.shape[1]
    total = branch.shape[0]
    group = total // batches
    half = group // 2
    rows = group // n
    names = gather_names(n, batches)
    for k in range(count):
        size = pieces[k].shape[0]
        branch[k * size : (k + 1) * size, :] = pieces[k][...]
    for c in range(2):
        for m in range(batches):
            k = c * batches + m
            at = slice(k * half, (k + 1) * half)
            gated = mt(branch[at, :], out_ref[...])
            for j, e in enumerate(names[m]):
                other = me[0] ^ (2 * e + c)
                at = m * group + other * rows
                natural[pl.ds(pl.multiple_of(at, 8), rows), :] = gated[j * rows : (j + 1) * rows]
    totals = [jnp.zeros((1, taps.shape[1]), F32)] * 3
    for m in range(batches):
        gated = natural[m * group : (m + 1) * group, :]
        place = offset[m]
        wide = p_nat[m].astype(F32)
        grad = gated * c_nat[m]
        grad_c = (gated * conv[m]).astype(BF16)
        one = jnp.where(place >= 1, grad, 0.0)
        two = jnp.where(place >= 2, grad, 0.0)
        totals[0] += jnp.sum(two * pltpu.roll(wide, 2, 0), axis=0, keepdims=True)
        totals[1] += jnp.sum(one * pltpu.roll(wide, 1, 0), axis=0, keepdims=True)
        totals[2] += jnp.sum(grad * wide, axis=0, keepdims=True)
        d_product = (
            grad * taps[2:3, :]
            + pltpu.roll(one, group - 1, 0) * taps[1:2, :]
            + pltpu.roll(two, group - 2, 0) * taps[0:1, :]
        ).astype(BF16)
        lines = lax.broadcasted_iota(jnp.int32, (group, group), 0)
        undeal = (source[m] == lines).astype(F32).astype(BF16)
        d_prod = mm(undeal, d_product)
        c_back = mm(undeal, grad_c)
        for c in range(2):
            there = pl.ds((c * batches + m) * half, half)
            piece = d_prod[c * half : (c + 1) * half]
            d_proj[there, :channels] = (piece * x_arr[there, :]).astype(BF16)
            d_proj[there, channels : 2 * channels] = c_back[c * half : (c + 1) * half].astype(BF16)
            d_proj[there, 2 * channels :] = (piece * b_arr[there, :]).astype(BF16)
    for k in range(3):
        conv_grad[k : k + 1, :] = totals[k]
    lanes = lax.broadcasted_iota(jnp.int32, (slot.shape[0], total), 1)
    picked = (slot[...] == lanes).astype(F32).astype(BF16)
    own[...] = mm(picked, branch[...]).astype(BF16)


def final_kernel(batches, n_dp, z, tokens, gain, d_hidden, *refs):
    terms, out = refs[:-1], refs[-1]
    back = exchange(summed(batches, terms), z[0], n_dp, True)
    wide = tokens[...].astype(F32)
    inv = lax.rsqrt(jnp.mean(wide * wide, axis=1, keepdims=True) + EPS)
    unit = wide * inv
    scaled = back * gain[...]
    mean = jnp.mean(scaled * unit, axis=1, keepdims=True)
    out[...] = (d_hidden[...].astype(F32) + inv * (scaled - unit * mean)).astype(BF16)


def block_kernel(batches, hidden, *refs):
    terms, out = refs[:-1], refs[-1]
    out[...] = (hidden[...] + summed(batches, terms)).astype(BF16)


def body(
    tokens_in,
    in_weight,
    conv_weight,
    out_weight,
    norm_gain,
    ff_gain,
    gate_weight,
    up_weight,
    down_weight,
    cotangent,
    deal_table,
    seq_lengths,
):
    batches, rows_dev, width = tokens_in.shape
    n, n_dp = lax.axis_size("shard"), lax.axis_size("dp")
    half = n // 2
    me, z = lax.axis_index("shard"), lax.axis_index("dp")
    group = n * rows_dev
    piece_rows = rows_dev // n
    own_rows, hidden_units = gate_weight.shape
    total = batches * group
    outer = bits_of(n)[1:]
    zblock = n * own_rows
    channels = n_dp * own_rows

    whole = hidden_units // (LANES * n) * LANES
    rest = hidden_units // n - whole

    place = jnp.arange(zblock, dtype=jnp.int32)
    identity = (place[:, None] == place[None, :]).astype(BF16)
    own_total = batches * rows_dev
    share = hidden_units // n
    chunk = total // 4
    cut = width // 2
    names = gather_names(n, batches)

    def dealt(blocks):
        return lax.all_to_all(blocks, "shard", split_axis=0, concat_axis=0, tiled=True)

    def flipped(block):
        return dot(block.reshape(zblock, -1), identity, ((0,), (0,)), BF16)

    in_parts = in_weight.reshape(own_rows, 3 * n_dp, n, own_rows).transpose(2, 0, 1, 3)
    in_parts = in_parts.reshape(n, own_rows, 3 * channels)
    spare = 14
    table = deal_table[:, 0, 0, :].astype(BF16).reshape(-1)
    table = jnp.pad(table, (0, own_rows * spare - table.shape[0])).reshape(own_rows, spare)
    extra = jnp.concatenate([norm_gain[:, None], ff_gain[:, None], table], axis=1)
    in_parts = jnp.concatenate([in_parts, jnp.broadcast_to(extra[None], (n,) + extra.shape)], axis=2)
    in_came = dealt(in_parts)
    tok_turned = turned(after(tokens_in, in_parts), z, n_dp)
    tok_pieces, tok_steps = plane_gather([tok_turned[m] for m in range(batches)])
    out_aug = jnp.concatenate(
        [out_weight, conv_weight, jnp.zeros((own_rows, LANES - conv_weight.shape[1]), BF16)], axis=1
    )
    out_lines = out_aug
    out_steps = []
    for bit in reversed(bits_of(n_dp)):
        out_came = swap(out_lines, bit, "dp")
        out_steps.append(out_came)
        if bit > 1:
            out_lines = jnp.concatenate([out_lines, out_came], axis=0)

    weights = [gate_weight, up_weight, down_weight]
    [ff_parts] = run(
        functools.partial(spread_kernel, n, whole, rest, 3),
        [((n, 3 * own_rows, share), BF16)],
        [],
        weights,
    )
    ff_came = dealt(after(ff_parts, in_came, *tok_steps[0], out_steps[0]))
    out_full, tap_cols = run(
        functools.partial(out_kernel, n_dp),
        [((channels, width), BF16), ((channels, LANES), BF16)],
        [z],
        [out_lines, out_came],
    )
    taps = tap_cols[:, : conv_weight.shape[1]].astype(F32).T

    deal = in_came[:, :, 3 * channels + 2 :].reshape(n, own_rows * spare)[:, : batches * n]
    deal = deal.reshape(n, batches, n).transpose(1, 0, 2).astype(jnp.int32)
    m_index = jnp.arange(batches, dtype=jnp.int32)[:, None, None, None]
    j_index = jnp.arange(n, dtype=jnp.int32)[None, :, None, None]
    t_index = jnp.arange(piece_rows, dtype=jnp.int32)[None, None, None, :]

    def place_of(e, m):
        out = jnp.zeros_like(e + m)
        for part in range(batches):
            for k, name in enumerate(names[part]):
                out = jnp.where((e == name) & (m == part), k, out)
        return out

    def within(m, holder, row):
        rel = holder ^ me
        return ((rel & 1) * half + place_of(rel >> 1, m)) * rows_dev + row

    def arrival_row(m, holder, row):
        rel = holder ^ me
        return (((rel & 1) * batches + m) * half + place_of(rel >> 1, m)) * rows_dev + row

    slot_row = j_index * piece_rows + t_index
    source = within(m_index, deal[:, :, :, None], slot_row).reshape(batches, group)
    own_deal = lax.dynamic_index_in_dim(deal, me, 1, keepdims=True)[:, :, :, None]
    own_source = arrival_row(m_index, own_deal, me * piece_rows + t_index).reshape(own_total, 1)
    inverse = jnp.sum(jnp.where(deal == me, jnp.arange(n, dtype=jnp.int32)[None, None, :], 0), axis=2)
    slot_source = arrival_row(
        m_index[:, :, 0], j_index[:, :, 0], inverse[:, :, None] * piece_rows + t_index[:, 0]
    ).reshape(own_total, 1)

    lengths = seq_lengths[:, 0, :]
    places = jnp.arange(group, dtype=jnp.int32)
    seq_start = jnp.zeros((batches, group), jnp.int32)
    start = jnp.zeros((batches,), jnp.int32)
    for k in range(lengths.shape[1]):
        seq_start = jnp.where(start[:, None] <= places[None, :], start[:, None], seq_start)
        start = start + lengths[:, k]
    offset = (places[None, :] - seq_start)[:, :, None]

    waits = (*tok_pieces, out_full, taps, source, own_source, slot_source, offset)
    in_a, in_b = line_gather(flipped(in_came), ((), waits))
    gate_block, up_block = [flipped(ff_came[:, k * own_rows : (k + 1) * own_rows]) for k in range(2)]
    two_block = after(jnp.concatenate([gate_block, up_block], axis=0), in_b)
    two = lax.all_gather(two_block, "dp", axis=1, tiled=True)

    def natural_row(row):
        both = jnp.concatenate([in_a[row : row + 1], in_b[row : row + 1]], axis=1)
        step = width // n_dp
        out = None
        for k in range(n_dp):
            order = [reversed_bits(k ^ p, n_dp) for p in range(n_dp)]
            moved = jnp.concatenate([both[:, q * step : (q + 1) * step] for q in order], axis=1)
            out = moved if out is None else jnp.where(z == k, moved, out)
        return out.astype(F32)

    gain_one = natural_row(3 * channels)
    gain_two = natural_row(3 * channels + 1)
    arr = (total, channels)
    nat = (batches, group, channels)
    own = (own_total, width)
    side = (total, cut)
    normed_a, normed_b, made, c_high, c_low, b_arr, x_arr, own_tok = run(
        functools.partial(project_kernel, channels, len(tok_pieces)),
        [(side, BF16), (side, BF16), (arr, BF16), (arr, BF16), (arr, BF16), (arr, F32), (arr, F32), (own, BF16)],
        [],
        [*tok_pieces, in_a, in_b, own_source],
        [pltpu.VMEM((total, width), BF16)],
    )
    p_nat, c_nat, conv_out, gated_arr = run(
        functools.partial(conv_kernel, batches, n),
        [(nat, BF16), (nat, F32), (nat, F32), (arr, BF16)],
        [me],
        [made, c_high, c_low, source[:, :, None], offset, taps],
        [pltpu.VMEM((group, channels), F32)],
    )
    down_block = flipped(after(ff_came, gated_arr)[:, 2 * own_rows :])
    down = lax.all_gather(down_block, "dp", axis=1, tiled=True)
    cot_pieces, cot_steps = plane_gather([cotangent[m] for m in range(batches)], ((ff_came, *tok_steps[-1]), ()))

    def summed_rows(lhs, rhs, wait=()):
        far = half_rows(lhs, rhs, 1, BF16, 2 * batches)
        [near] = half_rows(lhs, rhs, 0, F32, 1)
        return plane_reduce(near, [swap(piece, 1) for piece in far], batches, wait)[0]

    mine = ((rows_dev, width), BF16)
    hidden, unit_two, *ff_own = run(
        functools.partial(hidden_kernel, batches, n_dp),
        [(own, F32), (own, F32)] + [mine] * batches,
        [z],
        [own_tok, gain_two, *summed_rows(gated_arr, [out_full], cot_steps[-1])],
    )
    ff_pieces, ff_steps = plane_gather(ff_own)
    whole_rows = ((total, width), BF16)
    [cot_all] = run(functools.partial(stack_kernel, len(cot_pieces)), [whole_rows], [], cot_pieces)

    ff = (total, share)
    lean, ff_inner, by_gate, by_up = run(
        functools.partial(gate_kernel, len(ff_pieces)),
        [whole_rows, (ff, BF16), (ff, BF16), (ff, BF16)],
        [],
        [*ff_pieces, two],
    )

    def line_sum(former, latter, wait=()):
        value = after(product(former, latter, 4), *wait)
        return lax.psum_scatter(value, "dp", scatter_dimension=0, tiled=True)

    turn = functools.partial(columns_kernel, width // 6)
    [cot_columns] = run(turn, [((width, total), BF16)], [], [cot_all])
    [lean_columns] = run(turn, [((width, total), BF16)], [], [lean])
    down_sum = line_sum(cot_columns, ff_inner)
    d_far = inner_half(1, chunk, cot_all, down, by_gate, by_up)
    far = half_rows(d_far, [two], 1, BF16, 2 * batches)
    came = [swap(piece, 1) for piece in far]
    d_two = inner_half(0, chunk, after(cot_all, *far), down, by_gate, by_up, d_far)
    [near] = half_rows(after(d_two, *came), [two], 0, F32, 1)
    d_ff, first_came = plane_reduce(near, came, batches)
    two_sum = line_sum(lean_columns, d_two, first_came)
    cot_own = cotangent.reshape(own)
    branch_own = run(
        functools.partial(branch_kernel, batches),
        [mine] * batches,
        [],
        [cot_own, hidden, unit_two, gain_two, *d_ff],
    )
    branch_pieces, branch_steps = plane_gather(branch_own)

    block_came = [swap(piece, 1) for piece in half_rows(ff_inner, [down], 1, BF16, 2 * batches)]
    [block_near] = half_rows(ff_inner, [down], 0, F32, 1)
    branch_pieces[0] = after(branch_pieces[0], block_near, *block_came)

    branch, d_proj, conv_term, d_hidden_own = run(
        functools.partial(conv_back_kernel, batches, n, len(branch_pieces)),
        [whole_rows, ((total, 3 * channels), BF16), ((3, channels), F32), (own, BF16)],
        [me],
        [
            *branch_pieces,
            out_full,
            conv_out,
            c_nat,
            p_nat,
            b_arr,
            x_arr,
            source[:, None, :],
            offset,
            slot_source,
            taps,
        ],
        [pltpu.VMEM((total, channels), F32)],
    )
    in_sides = [in_a[: 3 * channels], in_b[: 3 * channels]]
    down_back = dealt(down_sum.reshape(n, own_rows, -1))
    d_normed = summed_rows(d_proj, in_sides, (down_back,))
    block_sum, _ = plane_reduce(block_near, block_came, batches, d_normed[batches:])
    [block_out] = run(functools.partial(block_kernel, batches), [(own, BF16)], [], [hidden, *block_sum])
    block_out = block_out.reshape(tokens_in.shape)
    [tokens_grad] = run(
        functools.partial(final_kernel, batches, n_dp),
        [(own, BF16)],
        [z],
        [tokens_in.reshape(own), gain_one, d_hidden_own, *d_normed],
    )
    tokens_grad = tokens_grad.reshape(tokens_in.shape)

    conv_cols = jnp.pad(conv_term.T, ((0, 0), (0, LANES - conv_term.shape[0])))
    keep, send = run(
        functools.partial(relative_kernel, n_dp),
        [((channels // 2, width + LANES), F32), ((channels // 2, width + LANES), BF16)],
        [z],
        [dot(gated_arr, branch, ((0,), (0,))), conv_cols],
    )
    out_came = []
    for bit in bits_of(n_dp):
        came = swap(send, bit, "dp")
        out_came.append(came)
        keep = keep + came.astype(F32)
        if 2 * bit < n_dp:
            keep, send = jnp.split(keep, 2, axis=0)
            send = after(send.astype(BF16), *d_normed[batches:])
    in_sum = line_reduce(dot(normed_a, d_proj, ((0,), (0,))), dot(normed_b, d_proj, ((0,), (0,)), BF16), (*d_normed[batches:], out_came[0]))
    out_grad = keep[:, :width]
    conv_grad = keep[:, width : width + conv_weight.shape[1]]
    two_back = dealt(two_sum.reshape(n, own_rows, -1))
    in_total = (in_sum[0] + in_sum[1].astype(F32)).astype(BF16).reshape(n, own_rows, -1)
    in_back = dealt(after(in_total, two_back))

    def joined(kernel, came, *weights):
        outs = [((own_rows, 1), F32)] * (2 * len(weights))
        outs[::2] = [(weight.shape, F32) for weight in weights]
        return run(kernel, outs, [], [came, *weights])

    join = functools.partial(join_kernel, n, whole, rest)
    down_grad, _ = joined(functools.partial(join, 1), down_back, down_weight)
    gate_grad, gate_dots, up_grad, up_dots = joined(functools.partial(join, 2), two_back, gate_weight, up_weight)
    in_grad, in_dots = joined(functools.partial(join_in_kernel, n, 3 * n_dp), in_back, in_weight)
    norm_gain_grad = in_dots[:, 0] / norm_gain.astype(F32)
    ff_gain_grad = (gate_dots + up_dots)[:, 0] / ff_gain.astype(F32)
    return (
        block_out,
        tokens_grad,
        in_grad,
        conv_grad,
        out_grad,
        norm_gain_grad,
        ff_gain_grad,
        gate_grad,
        up_grad,
        down_grad,
    )


def solution(mesh):
    rows = P(("dp", "shard"), None)
    tokens = P(None, ("dp", "shard"), None)
    vector = P(("dp", "shard"))
    placed = (
        tokens,
        rows,
        rows,
        rows,
        vector,
        vector,
        rows,
        rows,
        rows,
        tokens,
        P(None, "dp", "shard", None),
        P(None, "dp", None),
    )
    return jax.shard_map(
        body,
        mesh=mesh,
        in_specs=placed,
        out_specs=(tokens, tokens, rows, rows, rows, vector, vector, rows, rows, rows),
        check_vma=False,
    )
```

```python
import functools

import jax
import jax.numpy as jnp
from jax import lax
from jax.experimental import pallas as pl
from jax.experimental.pallas import tpu as pltpu
from jax.sharding import PartitionSpec as P

EPS = 1e-05
F32 = jnp.float32
BF16 = jnp.bfloat16
LANES = 128


def dot(former, latter, dims, out=F32):
    return lax.dot_general(
        former, latter, ((dims[0], dims[1]), ((), ())), preferred_element_type=F32
    ).astype(out)


def bits_of(count):
    return [1 << k for k in range(count.bit_length() - 1)]


def swap(value, bit, axis="shard"):
    n = lax.axis_size(axis)
    return lax.ppermute(value, axis, [(i, i ^ bit) for i in range(n)])


def route(outer, turn):
    turn = turn % len(outer)
    return outer[turn:] + outer[:turn]


def after(value, *others):
    others = [other for other in others if other is not None]
    if not others:
        return value
    return lax.optimization_barrier((value, *others))[0]


def gather_names(n, parts):
    outer = bits_of(n)[1:]
    names = []
    for m in range(parts):
        order = [0]
        for bit in route(outer, m):
            order = order + [e ^ (bit >> 1) for e in order]
        names.append(order)
    return names


def plane_gather(parts, waits=((), ())):
    n = lax.axis_size("shard")
    outer = bits_of(n)[1:]
    held = [[part] for part in parts]
    steps = []
    for k in range(len(outer)):
        going = [h[0] if len(h) == 1 else jnp.concatenate(h, axis=0) for h in held]
        if k < len(waits):
            going = [after(g, *waits[k]) for g in going]
        came = [swap(going[m], route(outer, m)[k]) for m in range(len(parts))]
        held = [[g, c] for g, c in zip(going, came)]
        steps.append(tuple(came))
    near = [piece for h in held for piece in h]
    far = [swap(piece, 1) for piece in near]
    return near + far, steps


def fold_kernel(rows, plans, *refs):
    count = len(plans)
    kept, came, sends, keeps = (refs[k * count : (k + 1) * count] for k in range(4))
    for m, (going, staying) in enumerate(plans):
        for out, places in ((sends[m], going), (keeps[m], staying)):
            for k, place in enumerate(places):
                at = slice(place * rows, (place + 1) * rows)
                value = kept[m][at, :] + came[m][at, :].astype(F32)
                out[k * rows : (k + 1) * rows, :] = value.astype(out.dtype)


def first_fold_kernel(rows, plans, near, *refs):
    count = len(plans)
    came, sends, keeps = refs[: len(refs) - 2 * count], refs[len(refs) - 2 * count : -count], refs[-count:]
    per = came[0].shape[0] // rows
    for m, (going, staying) in enumerate(plans):
        for out, places in ((sends[m], going), (keeps[m], staying)):
            for k, place in enumerate(places):
                at = slice(place * rows, (place + 1) * rows)
                there = slice(place % per * rows, (place % per + 1) * rows)
                value = near[at, :] + came[place // per][there, :].astype(F32)
                out[k * rows : (k + 1) * rows, :] = value.astype(out.dtype)


def plane_reduce(near, came, parts, wait=(), late=()):
    n = lax.axis_size("shard")
    half = n // 2
    outer = bits_of(n)[1:]
    width = near.shape[1]
    rows = near.shape[0] // (parts * half)
    names = gather_names(n, parts)
    kept, arrived = near, came
    for k in reversed(range(len(outer))):
        plans = []
        for m in range(parts):
            bit = route(outer, m)[k] >> 1
            going = [e for e in names[m] if e & bit]
            base = m * half if kept is near else 0
            plans.append(([base + names[m].index(e) for e in going], [base + names[m].index(e ^ bit) for e in going]))
            names[m] = [e ^ bit for e in going]
        shape = (len(plans[0][0]) * rows, width)
        outs = [(shape, BF16)] * parts + [(shape, F32)] * parts
        if kept is near:
            made = run(functools.partial(first_fold_kernel, rows, plans), outs, [], [near, *came])
            sends = [after(send, *wait) for send in made[:parts]]
        else:
            made = run(functools.partial(fold_kernel, rows, plans), outs, [], [*kept, *arrived])
            sends = [after(send, *late) for send in made[:parts]]
        first = kept is near
        kept = made[parts:]
        arrived = [swap(sends[m], route(outer, m)[k]) for m in range(parts)]
        if first:
            first_came = arrived
    return [*kept, *arrived], first_came


def line_gather(block, waits=((), ())):
    n = lax.axis_size("dp")
    block = after(block, *waits[0])
    first = None
    for bit in reversed(bits_of(n)):
        came = swap(block, bit, "dp")
        first = came if first is None else first
        if bit == 1:
            return block, came, first
        block = after(jnp.concatenate([block, came], axis=1), *waits[1])


def line_reduce(keep, send, wait=()):
    n = lax.axis_size("dp")
    for bit in bits_of(n):
        came = swap(send, bit, "dp")
        if 2 * bit == n:
            return keep, came
        total = keep + came.astype(F32)
        cut = total.shape[0] // 2
        keep, send = total[:cut], after(total[cut:].astype(BF16), *wait)


def reversed_bits(index, n):
    out = 0
    for k, bit in enumerate(bits_of(n)):
        if index & bit:
            out |= n >> (k + 1)
    return out


def turned(value, z, n):
    step = value.shape[-1] // n
    pieces = [value[..., k * step : (k + 1) * step] for k in range(n)]
    out = None
    for k in range(n):
        order = [pieces[k ^ reversed_bits(p, n)] for p in range(n)]
        moved = jnp.concatenate(order, axis=-1)
        out = moved if out is None else jnp.where(z == k, moved, out)
    return out


def exchange(value, z, n, back):
    step = value.shape[1] // n
    pieces = [value[:, p * step : (p + 1) * step] for p in range(n)]

    def reorder(pieces):
        return [pieces[reversed_bits(p, n)] for p in range(n)]

    def flip(pieces):
        for k, bit in enumerate(bits_of(n)):
            low = n >> (k + 1)
            pieces = [jnp.where((z & bit) != 0, pieces[p ^ low], pieces[p]) for p in range(n)]
        return pieces

    return jnp.concatenate(reorder(flip(pieces)) if back else flip(reorder(pieces)), axis=1)


WHOLE = pl.BlockSpec(memory_space=pltpu.VMEM)
SCALAR = pl.BlockSpec(memory_space=pltpu.SMEM)


def run(kernel, outs, scalars, arrays, scratch=()):
    return pl.pallas_call(
        kernel,
        out_shape=[jax.ShapeDtypeStruct(shape, dtype) for shape, dtype in outs],
        in_specs=[SCALAR] * len(scalars) + [WHOLE] * len(arrays),
        out_specs=[WHOLE] * len(outs),
        scratch_shapes=list(scratch),
        compiler_params=pltpu.CompilerParams(vmem_limit_bytes=2 * lax.axis_size("shard") * 2**20),
        cost_estimate=pl.CostEstimate(flops=1000, bytes_accessed=1000, transcendentals=0),
    )(*[jnp.asarray(v, jnp.int32).reshape(1) for v in scalars], *arrays)


def mm(former, latter):
    return lax.dot_general(former, latter, (((1,), (0,)), ((), ())), preferred_element_type=F32)


def mt(former, latter):
    return lax.dot_general(former, latter, (((1,), (1,)), ((), ())), preferred_element_type=F32)


def spread_kernel(n, whole, rest, count, *refs):
    weights, out = refs[:count], refs[count]
    rows = weights[0].shape[0]
    for k in range(count):
        for s in range(n):
            at = slice(k * rows, (k + 1) * rows)
            first = n * whole + s * rest
            out[s, at, :whole] = weights[k][:, s * whole : (s + 1) * whole]
            out[s, at, whole:] = weights[k][:, first : first + rest]


def join_kernel(n, whole, rest, count, came, *refs):
    weights, outs = refs[:count], refs[count:]
    share = whole + rest
    for k in range(count):
        grad, dots = outs[2 * k : 2 * k + 2]
        first = k * share
        tails = [came[s, :, first + whole : first + share] for s in range(n)]
        grad[:, n * whole :] = jnp.concatenate(tails, axis=1).astype(F32)
        for s in range(n):
            grad[:, s * whole : (s + 1) * whole] = came[s, :, first : first + whole].astype(F32)
        dots[...] = jnp.sum(grad[...] * weights[k][...].astype(F32), axis=1, keepdims=True)


def join_in_kernel(n, groups, came, weight, grad, dots):
    rows = came.shape[1]
    for g in range(groups):
        piece = jnp.concatenate([came[s, :, g * rows : (g + 1) * rows] for s in range(n)], axis=1)
        grad[:, g * n * rows : (g + 1) * n * rows] = piece.astype(F32)
    dots[...] = jnp.sum(grad[...] * weight[...].astype(F32), axis=1, keepdims=True)


def by_line(pieces, z, n):
    for k, bit in enumerate(bits_of(n)):
        low = n >> (k + 1)
        pieces = [jnp.where((z & bit) != 0, pieces[p ^ low], pieces[p]) for p in range(n)]
    return [pieces[reversed_bits(p, n)] for p in range(n)]


def out_kernel(n, z, first, second, full, tap_cols):
    rows = first.shape[0] // (n // 2)
    width = full.shape[1]
    pieces = [(first, second)[p // (n // 2)][p % (n // 2) * rows : (p % (n // 2) + 1) * rows, :] for p in range(n)]
    for p, piece in enumerate(by_line(pieces, z[0], n)):
        at = slice(p * rows, (p + 1) * rows)
        full[at, :] = piece[:, :width]
        tap_cols[at, :] = piece[:, width:]


def relative_kernel(n, z, term, conv_term, keep, send):
    rows = term.shape[0] // n
    width = term.shape[1]
    for value, lanes in ((term, slice(0, width)), (conv_term, slice(width, None))):
        pieces = [value[reversed_bits(p, n) * rows : (reversed_bits(p, n) + 1) * rows, :] for p in range(n)]
        for k, bit in enumerate(bits_of(n)):
            low = n >> (k + 1)
            pieces = [jnp.where((z[0] & bit) != 0, pieces[p ^ low], pieces[p]) for p in range(n)]
        for p in range(n):
            out = (keep, send)[p // (n // 2)]
            at = slice(p % (n // 2) * rows, (p % (n // 2) + 1) * rows)
            out[at, lanes] = pieces[p].astype(out.dtype)


def stack_kernel(count, *refs):
    pieces, out = refs[:count], refs[count]
    rows = pieces[0].shape[0]
    for k in range(count):
        out[k * rows : (k + 1) * rows, :] = pieces[k][...]


def product_kernel(former, latter, out):
    out[...] = mm(former[...], latter[...]).astype(out.dtype)


def product(former, latter, blocks):
    rows = former.shape[0] // blocks
    return pl.pallas_call(
        product_kernel,
        out_shape=jax.ShapeDtypeStruct((former.shape[0], latter.shape[1]), BF16),
        grid=(blocks,),
        in_specs=[
            pl.BlockSpec((rows, former.shape[1]), lambda i: (i, 0)),
            pl.BlockSpec(latter.shape, lambda i: (0, 0)),
        ],
        out_specs=pl.BlockSpec((rows, latter.shape[1]), lambda i: (i, 0)),
        compiler_params=pltpu.CompilerParams(vmem_limit_bytes=48 * 2**20),
        cost_estimate=pl.CostEstimate(flops=1000, bytes_accessed=1000, transcendentals=0),
    )(former, latter)


def columns_kernel(chunk, rows, out):
    for k in range(rows.shape[1] // chunk):
        at = slice(k * chunk, (k + 1) * chunk)
        out[at, :] = rows[:, at].astype(F32).T.astype(BF16)


def project_kernel(channels, count, *refs):
    pieces = refs[:count]
    in_a, in_b, own_ref, normed_a, normed_b, product, c_high, c_low, b_out, x_out, own_tok = refs[count : count + 11]
    tok = refs[count + 11]
    rows = pieces[0].shape[0]
    split = in_a.shape[1]
    at_gain = 3 * channels
    gain = jnp.concatenate([in_a[at_gain : at_gain + 1, :], in_b[at_gain : at_gain + 1, :]], axis=1).astype(F32)
    for k in range(0, count, 2):
        at = slice(k * rows, (k + 2) * rows)
        for j in range(2):
            piece = pieces[k + j][...]
            here = slice((k + j) * rows, (k + j + 1) * rows)
            tok[here, :] = piece
            wide = piece.astype(F32)
            unit = wide * lax.rsqrt(jnp.mean(wide * wide, axis=1, keepdims=True) + EPS)
            lean = (unit * gain).astype(BF16)
            normed_a[here, :] = lean[:, :split]
            normed_b[here, :] = lean[:, split:]
        left, right = normed_a[at, :], normed_b[at, :]

        def part(j):
            lines = slice(j * channels, (j + 1) * channels)
            return mt(left, in_a[lines, :]) + mt(right, in_b[lines, :])

        b_part, c_part, x_part = part(0), part(1), part(2)
        high = c_part.astype(BF16)
        product[at, :] = (b_part * x_part).astype(BF16)
        c_high[at, :] = high
        c_low[at, :] = (c_part - high.astype(F32)).astype(BF16)
        b_out[at, :] = b_part
        x_out[at, :] = x_part
    lanes = lax.broadcasted_iota(jnp.int32, (own_ref.shape[0], tok.shape[0]), 1)
    own_tok[...] = mm((own_ref[...] == lanes).astype(F32).astype(BF16), tok[...]).astype(BF16)


def conv_kernel(batches, n, me, product, c_high, c_low, source, offset, taps, p_out, c_out, conv_out, gated_out, gated):
    names = gather_names(n, batches)
    group = source.shape[1]
    half = group // 2
    rows = group // n
    for m in range(batches):
        lanes = lax.broadcasted_iota(jnp.int32, (group, group), 1)
        deal = (source[m] == lanes).astype(F32).astype(BF16)
        first, second = pl.ds(m * half, half), pl.ds((batches + m) * half, half)

        def moved(ref):
            return mm(deal[:, :half], ref[first, :]) + mm(deal[:, half:], ref[second, :])

        wide = moved(product)
        c_part = moved(c_high) + moved(c_low)
        place = offset[m]
        prev_one = jnp.where(place >= 1, pltpu.roll(wide, 1, 0), 0.0)
        prev_two = jnp.where(place >= 2, pltpu.roll(wide, 2, 0), 0.0)
        conv = prev_two * taps[0:1, :] + prev_one * taps[1:2, :] + wide * taps[2:3, :]
        p_out[m] = wide.astype(BF16)
        c_out[m] = c_part
        conv_out[m] = conv
        gated[...] = c_part * conv
        for c in range(2):
            for k, e in enumerate(names[m]):
                other = me[0] ^ (2 * e + c)
                block = gated[pl.ds(pl.multiple_of(other * rows, 8), rows), :]
                at = ((c * batches + m) * (n // 2) + k) * rows
                gated_out[at : at + rows, :] = block.astype(BF16)


def summed(batches, terms):
    return jnp.concatenate([terms[m][...] + terms[batches + m][...].astype(F32) for m in range(batches)], axis=0)


def hidden_kernel(batches, n_dp, z, own_tok, gain, *refs):
    terms, (hidden, unit_out, *parts) = refs[: 2 * batches], refs[2 * batches :]
    value = exchange(own_tok[...].astype(F32), z[0], n_dp, True) + summed(batches, terms)
    hidden[...] = value
    unit = value * lax.rsqrt(jnp.mean(value * value, axis=1, keepdims=True) + EPS)
    unit_out[...] = unit
    lean = (unit * gain[...]).astype(BF16)
    rows = parts[0].shape[0]
    for m in range(batches):
        parts[m][...] = lean[m * rows : (m + 1) * rows]


def gate_kernel(count, *refs):
    pieces = refs[:count]
    two, lean, inner, by_gate, by_up = refs[count:]
    rows = pieces[0].shape[0]
    share = two.shape[0] // 2
    for k in range(0, count, 2):
        at = slice(k * rows, (k + 2) * rows)
        for j in range(2):
            lean[(k + j) * rows : (k + j + 1) * rows, :] = pieces[k + j][...]
        part = lean[at, :]
        gate = mt(part, two[:share, :])
        up = mt(part, two[share:, :])
        sig = jax.nn.sigmoid(gate)
        silu = gate * sig
        inner[at, :] = (silu * up).astype(BF16)
        by_gate[at, :] = (up * sig * (1.0 + gate * (1.0 - sig))).astype(BF16)
        by_up[at, :] = silu.astype(BF16)


def inner_kernel(chunk, cot, down, by_gate, by_up, *refs):
    d_two = refs[-1]
    share = by_gate.shape[1]
    for k in range(cot.shape[0] // chunk):
        at = slice(k * chunk, (k + 1) * chunk)
        d_inner = mt(cot[at, :], down[...])
        d_two[at, :share] = (d_inner * by_gate[at, :].astype(F32)).astype(BF16)
        d_two[at, share:] = (d_inner * by_up[at, :].astype(F32)).astype(BF16)


def inner_half(part, chunk, cot, down, by_gate, by_up, other=None):
    total, share = by_gate.shape

    def rows_of(width):
        return pl.BlockSpec((total // 2, width), lambda i: (part, 0))

    extra = [] if other is None else [other]
    return pl.pallas_call(
        functools.partial(inner_kernel, chunk),
        out_shape=jax.ShapeDtypeStruct((total, 2 * share), BF16),
        grid=(1,),
        in_specs=[rows_of(cot.shape[1]), pl.BlockSpec(down.shape, lambda i: (0, 0)), rows_of(share), rows_of(share)]
        + [pl.BlockSpec(memory_space=pl.ANY)] * len(extra),
        out_specs=rows_of(2 * share),
        input_output_aliases={4: 0} if extra else {},
        compiler_params=pltpu.CompilerParams(vmem_limit_bytes=48 * 2**20),
        cost_estimate=pl.CostEstimate(flops=1000, bytes_accessed=1000, transcendentals=0),
    )(cot, down, by_gate, by_up, *extra)


def rows_kernel(*refs, sides):
    lhs, rhs, outs = refs[0], refs[1 : 1 + sides], refs[1 + sides :]
    rows = outs[0].shape[0]
    per = max(1, 384 // rows)
    step = min(rows, 384)
    for k in range(0, len(outs), per):
        count = min(per, len(outs) - k)
        for first in range(0, rows, step):
            at = slice(k * rows + first, k * rows + first + step * count)
            for j in range(sides):
                split = rhs[j].shape[1]
                value = mm(lhs[at, :], rhs[j][...])
                for piece in range(count):
                    here = value[piece * step : (piece + 1) * step]
                    outs[k + piece][first : first + step, j * split : (j + 1) * split] = here.astype(outs[0].dtype)


def half_rows(lhs, rhs, part, dtype, pieces):
    rows = lhs.shape[0] // 2
    width = sum(side.shape[1] for side in rhs)
    shape = (rows // pieces, width)
    return pl.pallas_call(
        functools.partial(rows_kernel, sides=len(rhs)),
        out_shape=[jax.ShapeDtypeStruct(shape, dtype)] * pieces,
        grid=(1,),
        in_specs=[pl.BlockSpec((rows, lhs.shape[1]), lambda i: (part, 0))]
        + [pl.BlockSpec(side.shape, lambda i: (0, 0)) for side in rhs],
        out_specs=[pl.BlockSpec(shape, lambda i: (0, 0))] * pieces,
        compiler_params=pltpu.CompilerParams(vmem_limit_bytes=48 * 2**20),
        cost_estimate=pl.CostEstimate(flops=1000, bytes_accessed=1000, transcendentals=0),
    )(lhs, *rhs)


def branch_kernel(batches, cot, hidden, unit, gain, *refs):
    terms, parts = refs[: 2 * batches], refs[2 * batches :]
    value = hidden[...]
    inv = lax.rsqrt(jnp.mean(value * value, axis=1, keepdims=True) + EPS)
    scaled = summed(batches, terms) * gain[...]
    one = unit[...]
    mean = jnp.mean(scaled * one, axis=1, keepdims=True)
    lean = (cot[...].astype(F32) + inv * (scaled - one * mean)).astype(BF16)
    rows = parts[0].shape[0]
    for m in range(batches):
        parts[m][...] = lean[m * rows : (m + 1) * rows]


def conv_back_kernel(batches, n, count, me, *refs):
    pieces = refs[:count]
    out_ref, conv, c_nat, p_nat, b_arr, x_arr, source, offset, slot, taps = refs[count : count + 10]
    branch, d_proj, conv_grad, own, natural = refs[count + 10 :]
    channels = taps.shape[1]
    total = branch.shape[0]
    group = total // batches
    half = group // 2
    rows = group // n
    names = gather_names(n, batches)
    for k in range(count):
        size = pieces[k].shape[0]
        branch[k * size : (k + 1) * size, :] = pieces[k][...]
    for c in range(2):
        for m in range(batches):
            k = c * batches + m
            at = slice(k * half, (k + 1) * half)
            gated = mt(branch[at, :], out_ref[...])
            for j, e in enumerate(names[m]):
                other = me[0] ^ (2 * e + c)
                at = m * group + other * rows
                natural[pl.ds(pl.multiple_of(at, 8), rows), :] = gated[j * rows : (j + 1) * rows]
    totals = [jnp.zeros((1, taps.shape[1]), F32)] * 3
    for m in range(batches):
        gated = natural[m * group : (m + 1) * group, :]
        place = offset[m]
        wide = p_nat[m].astype(F32)
        grad = gated * c_nat[m]
        grad_c = (gated * conv[m]).astype(BF16)
        one = jnp.where(place >= 1, grad, 0.0)
        two = jnp.where(place >= 2, grad, 0.0)
        totals[0] += jnp.sum(two * pltpu.roll(wide, 2, 0), axis=0, keepdims=True)
        totals[1] += jnp.sum(one * pltpu.roll(wide, 1, 0), axis=0, keepdims=True)
        totals[2] += jnp.sum(grad * wide, axis=0, keepdims=True)
        d_product = (
            grad * taps[2:3, :]
            + pltpu.roll(one, group - 1, 0) * taps[1:2, :]
            + pltpu.roll(two, group - 2, 0) * taps[0:1, :]
        ).astype(BF16)
        lines = lax.broadcasted_iota(jnp.int32, (group, group), 0)
        undeal = (source[m] == lines).astype(F32).astype(BF16)
        d_prod = mm(undeal, d_product)
        c_back = mm(undeal, grad_c)
        for c in range(2):
            there = pl.ds((c * batches + m) * half, half)
            piece = d_prod[c * half : (c + 1) * half]
            d_proj[there, :channels] = (piece * x_arr[there, :]).astype(BF16)
            d_proj[there, channels : 2 * channels] = c_back[c * half : (c + 1) * half].astype(BF16)
            d_proj[there, 2 * channels :] = (piece * b_arr[there, :]).astype(BF16)
    for k in range(3):
        conv_grad[k : k + 1, :] = totals[k]
    lanes = lax.broadcasted_iota(jnp.int32, (slot.shape[0], total), 1)
    picked = (slot[...] == lanes).astype(F32).astype(BF16)
    own[...] = mm(picked, branch[...]).astype(BF16)


def final_kernel(batches, n_dp, z, tokens, gain, d_hidden, *refs):
    terms, out = refs[:-1], refs[-1]
    back = exchange(summed(batches, terms), z[0], n_dp, True)
    wide = tokens[...].astype(F32)
    inv = lax.rsqrt(jnp.mean(wide * wide, axis=1, keepdims=True) + EPS)
    unit = wide * inv
    scaled = back * gain[...]
    mean = jnp.mean(scaled * unit, axis=1, keepdims=True)
    out[...] = (d_hidden[...].astype(F32) + inv * (scaled - unit * mean)).astype(BF16)


def block_kernel(batches, hidden, *refs):
    terms, out = refs[:-1], refs[-1]
    out[...] = (hidden[...] + summed(batches, terms)).astype(BF16)


def body(
    tokens_in,
    in_weight,
    conv_weight,
    out_weight,
    norm_gain,
    ff_gain,
    gate_weight,
    up_weight,
    down_weight,
    cotangent,
    deal_table,
    seq_lengths,
):
    batches, rows_dev, width = tokens_in.shape
    n, n_dp = lax.axis_size("shard"), lax.axis_size("dp")
    half = n // 2
    me, z = lax.axis_index("shard"), lax.axis_index("dp")
    group = n * rows_dev
    piece_rows = rows_dev // n
    own_rows, hidden_units = gate_weight.shape
    total = batches * group
    outer = bits_of(n)[1:]
    zblock = n * own_rows
    channels = n_dp * own_rows

    whole = hidden_units // (LANES * n) * LANES
    rest = hidden_units // n - whole

    place = jnp.arange(zblock, dtype=jnp.int32)
    identity = (place[:, None] == place[None, :]).astype(BF16)
    own_total = batches * rows_dev
    share = hidden_units // n
    chunk = total // 4
    cut = width // 2
    names = gather_names(n, batches)

    def dealt(blocks):
        return lax.all_to_all(blocks, "shard", split_axis=0, concat_axis=0, tiled=True)

    def flipped(block):
        return dot(block.reshape(zblock, -1), identity, ((0,), (0,)), BF16)

    in_parts = in_weight.reshape(own_rows, 3 * n_dp, n, own_rows).transpose(2, 0, 1, 3)
    in_parts = in_parts.reshape(n, own_rows, 3 * channels)
    spare = 14
    table = deal_table[:, 0, 0, :].astype(BF16).reshape(-1)
    table = jnp.pad(table, (0, own_rows * spare - table.shape[0])).reshape(own_rows, spare)
    extra = jnp.concatenate([norm_gain[:, None], ff_gain[:, None], table], axis=1)
    in_parts = jnp.concatenate([in_parts, jnp.broadcast_to(extra[None], (n,) + extra.shape)], axis=2)
    in_came = dealt(in_parts)
    out_aug = jnp.concatenate(
        [out_weight, conv_weight, jnp.zeros((own_rows, LANES - conv_weight.shape[1]), BF16)], axis=1
    )
    out_lines = out_aug
    out_steps = []
    for bit in reversed(bits_of(n_dp)):
        out_came = swap(out_lines, bit, "dp")
        out_steps.append(out_came)
        if bit > 1:
            out_lines = jnp.concatenate([out_lines, out_came], axis=0)

    tok_turned = turned(after(tokens_in, in_parts), z, n_dp)
    tok_pieces, tok_steps = plane_gather([tok_turned[m] for m in range(batches)], ((), (out_steps[0],)))

    out_full, tap_cols = run(
        functools.partial(out_kernel, n_dp),
        [((channels, width), BF16), ((channels, LANES), BF16)],
        [z],
        [out_lines, out_came],
    )
    taps = tap_cols[:, : conv_weight.shape[1]].astype(F32).T

    deal = in_came[:, :, 3 * channels + 2 :].reshape(n, own_rows * spare)[:, : batches * n]
    deal = deal.reshape(n, batches, n).transpose(1, 0, 2).astype(jnp.int32)
    m_index = jnp.arange(batches, dtype=jnp.int32)[:, None, None, None]
    j_index = jnp.arange(n, dtype=jnp.int32)[None, :, None, None]
    t_index = jnp.arange(piece_rows, dtype=jnp.int32)[None, None, None, :]

    def place_of(e, m):
        out = jnp.zeros_like(e + m)
        for part in range(batches):
            for k, name in enumerate(names[part]):
                out = jnp.where((e == name) & (m == part), k, out)
        return out

    def within(m, holder, row):
        rel = holder ^ me
        return ((rel & 1) * half + place_of(rel >> 1, m)) * rows_dev + row

    def arrival_row(m, holder, row):
        rel = holder ^ me
        return (((rel & 1) * batches + m) * half + place_of(rel >> 1, m)) * rows_dev + row

    slot_row = j_index * piece_rows + t_index
    source = within(m_index, deal[:, :, :, None], slot_row).reshape(batches, group)
    own_deal = lax.dynamic_index_in_dim(deal, me, 1, keepdims=True)[:, :, :, None]
    own_source = arrival_row(m_index, own_deal, me * piece_rows + t_index).reshape(own_total, 1)
    inverse = jnp.sum(jnp.where(deal == me, jnp.arange(n, dtype=jnp.int32)[None, None, :], 0), axis=2)
    slot_source = arrival_row(
        m_index[:, :, 0], j_index[:, :, 0], inverse[:, :, None] * piece_rows + t_index[:, 0]
    ).reshape(own_total, 1)

    lengths = seq_lengths[:, 0, :]
    places = jnp.arange(group, dtype=jnp.int32)
    seq_start = jnp.zeros((batches, group), jnp.int32)
    start = jnp.zeros((batches,), jnp.int32)
    for k in range(lengths.shape[1]):
        seq_start = jnp.where(start[:, None] <= places[None, :], start[:, None], seq_start)
        start = start + lengths[:, k]
    offset = (places[None, :] - seq_start)[:, :, None]

    waits = (*tok_pieces, out_full, taps, source, own_source, slot_source, offset)
    in_a, in_b, in_first = line_gather(flipped(in_came), ((), waits))

    def spread(*weights):
        rows = sum(weight.shape[0] for weight in weights)
        kernel = functools.partial(spread_kernel, n, whole, rest, len(weights))
        return run(kernel, [((n, rows, share), BF16)], [], weights)[0]

    ff_came = dealt(after(spread(gate_weight, up_weight), in_first, *tok_steps[-1]))
    gate_block, up_block = [flipped(ff_came[:, k * own_rows : (k + 1) * own_rows]) for k in range(2)]
    two_block = after(jnp.concatenate([gate_block, up_block], axis=0), in_b)
    down_came = dealt(after(spread(down_weight), ff_came))
    two = lax.all_gather(two_block, "dp", axis=1, tiled=True)

    def natural_row(row):
        both = jnp.concatenate([in_a[row : row + 1], in_b[row : row + 1]], axis=1)
        step = width // n_dp
        out = None
        for k in range(n_dp):
            order = [reversed_bits(k ^ p, n_dp) for p in range(n_dp)]
            moved = jnp.concatenate([both[:, q * step : (q + 1) * step] for q in order], axis=1)
            out = moved if out is None else jnp.where(z == k, moved, out)
        return out.astype(F32)

    gain_one = natural_row(3 * channels)
    gain_two = natural_row(3 * channels + 1)
    arr = (total, channels)
    nat = (batches, group, channels)
    own = (own_total, width)
    side = (total, cut)
    normed_a, normed_b, made, c_high, c_low, b_arr, x_arr, own_tok = run(
        functools.partial(project_kernel, channels, len(tok_pieces)),
        [(side, BF16), (side, BF16), (arr, BF16), (arr, BF16), (arr, BF16), (arr, F32), (arr, F32), (own, BF16)],
        [],
        [*tok_pieces, in_a, in_b, own_source],
        [pltpu.VMEM((total, width), BF16)],
    )
    p_nat, c_nat, conv_out, gated_arr = run(
        functools.partial(conv_kernel, batches, n),
        [(nat, BF16), (nat, F32), (nat, F32), (arr, BF16)],
        [me],
        [made, c_high, c_low, source[:, :, None], offset, taps],
        [pltpu.VMEM((group, channels), F32)],
    )
    down_block = flipped(after(down_came, gated_arr))
    down = lax.all_gather(down_block, "dp", axis=1, tiled=True)
    cot_pieces, cot_steps = plane_gather([cotangent[m] for m in range(batches)], ((ff_came, *tok_steps[-1]), ()))

    def summed_rows(lhs, rhs, wait=()):
        far = half_rows(lhs, rhs, 1, BF16, 2 * batches)
        [near] = half_rows(lhs, rhs, 0, F32, 1)
        return plane_reduce(near, [swap(piece, 1) for piece in far], batches, wait)[0]

    mine = ((rows_dev, width), BF16)
    hidden, unit_two, *ff_own = run(
        functools.partial(hidden_kernel, batches, n_dp),
        [(own, F32), (own, F32)] + [mine] * batches,
        [z],
        [own_tok, gain_two, *summed_rows(gated_arr, [out_full], (*cot_steps[-1], down_came))],
    )
    ff_pieces, ff_steps = plane_gather(ff_own)
    whole_rows = ((total, width), BF16)
    [cot_all] = run(functools.partial(stack_kernel, len(cot_pieces)), [whole_rows], [], cot_pieces)

    ff = (total, share)
    lean, ff_inner, by_gate, by_up = run(
        functools.partial(gate_kernel, len(ff_pieces)),
        [whole_rows, (ff, BF16), (ff, BF16), (ff, BF16)],
        [],
        [*ff_pieces, two],
    )

    def line_sum(former, latter, wait=()):
        value = after(product(former, latter, 4), *wait)
        return lax.psum_scatter(value, "dp", scatter_dimension=0, tiled=True)

    turn = functools.partial(columns_kernel, width // 6)
    [cot_columns] = run(turn, [((width, total), BF16)], [], [cot_all])
    [lean_columns] = run(turn, [((width, total), BF16)], [], [lean])
    down_sum = line_sum(cot_columns, ff_inner)
    d_far = inner_half(1, chunk, cot_all, down, by_gate, by_up)
    far = half_rows(d_far, [two], 1, BF16, 2 * batches)
    came = [swap(piece, 1) for piece in far]
    d_two = inner_half(0, chunk, after(cot_all, *far), down, by_gate, by_up, d_far)
    [near] = half_rows(after(d_two, *came), [two], 0, F32, 1)
    d_ff, first_came = plane_reduce(near, came, batches)
    two_sum = line_sum(lean_columns, d_two, first_came)
    cot_own = cotangent.reshape(own)
    branch_own = run(
        functools.partial(branch_kernel, batches),
        [mine] * batches,
        [],
        [cot_own, hidden, unit_two, gain_two, *d_ff],
    )
    block_came = [swap(piece, 1) for piece in half_rows(ff_inner, [down], 1, BF16, 2 * batches)]
    [block_near] = half_rows(ff_inner, [down], 0, F32, 1)
    branch_pieces, branch_steps = plane_gather(branch_own, ((), (block_near,)))
    block_sum, block_first = plane_reduce(block_near, block_came, batches, branch_steps[-1])


    branch, d_proj, conv_term, d_hidden_own = run(
        functools.partial(conv_back_kernel, batches, n, len(branch_pieces)),
        [whole_rows, ((total, 3 * channels), BF16), ((3, channels), F32), (own, BF16)],
        [me],
        [
            *branch_pieces,
            out_full,
            conv_out,
            c_nat,
            p_nat,
            b_arr,
            x_arr,
            source[:, None, :],
            offset,
            slot_source,
            taps,
        ],
        [pltpu.VMEM((total, channels), F32)],
    )
    in_sides = [in_a[: 3 * channels], in_b[: 3 * channels]]
    down_back = dealt(after(down_sum, *branch_steps[-1]).reshape(n, own_rows, -1))
    far = half_rows(after(d_proj, *block_first), in_sides, 1, BF16, 2 * batches)
    [near] = half_rows(d_proj, in_sides, 0, F32, 1)
    d_normed, _ = plane_reduce(
        near, [swap(piece, 1) for piece in far], batches, (down_back, *block_sum[batches:])
    )
    [block_out] = run(functools.partial(block_kernel, batches), [(own, BF16)], [], [hidden, *block_sum])
    block_out = block_out.reshape(tokens_in.shape)
    [tokens_grad] = run(
        functools.partial(final_kernel, batches, n_dp),
        [(own, BF16)],
        [z],
        [tokens_in.reshape(own), gain_one, d_hidden_own, *d_normed],
    )
    tokens_grad = tokens_grad.reshape(tokens_in.shape)

    conv_cols = jnp.pad(conv_term.T, ((0, 0), (0, LANES - conv_term.shape[0])))
    keep, send = run(
        functools.partial(relative_kernel, n_dp),
        [((channels // 2, width + LANES), F32), ((channels // 2, width + LANES), BF16)],
        [z],
        [dot(gated_arr, branch, ((0,), (0,))), conv_cols],
    )
    out_came = []
    for bit in bits_of(n_dp):
        came = swap(send, bit, "dp")
        out_came.append(came)
        keep = keep + came.astype(F32)
        if 2 * bit < n_dp:
            keep, send = jnp.split(keep, 2, axis=0)
            send = after(send.astype(BF16), *d_normed[batches:])
    in_sum = line_reduce(dot(normed_a, d_proj, ((0,), (0,))), dot(normed_b, d_proj, ((0,), (0,)), BF16), (*d_normed[batches:], out_came[0]))
    out_grad = keep[:, :width]
    conv_grad = keep[:, width : width + conv_weight.shape[1]]
    two_back = dealt(two_sum.reshape(n, own_rows, -1))
    in_total = (in_sum[0] + in_sum[1].astype(F32)).astype(BF16).reshape(n, own_rows, -1)
    in_back = dealt(after(in_total, two_back))

    def joined(kernel, came, *weights):
        outs = [((own_rows, 1), F32)] * (2 * len(weights))
        outs[::2] = [(weight.shape, F32) for weight in weights]
        return run(kernel, outs, [], [came, *weights])

    join = functools.partial(join_kernel, n, whole, rest)
    down_grad, _ = joined(functools.partial(join, 1), down_back, down_weight)
    gate_grad, gate_dots, up_grad, up_dots = joined(functools.partial(join, 2), two_back, gate_weight, up_weight)
    in_grad, in_dots = joined(functools.partial(join_in_kernel, n, 3 * n_dp), in_back, in_weight)
    norm_gain_grad = in_dots[:, 0] / norm_gain.astype(F32)
    ff_gain_grad = (gate_dots + up_dots)[:, 0] / ff_gain.astype(F32)
    return (
        block_out,
        tokens_grad,
        in_grad,
        conv_grad,
        out_grad,
        norm_gain_grad,
        ff_gain_grad,
        gate_grad,
        up_grad,
        down_grad,
    )


def solution(mesh):
    rows = P(("dp", "shard"), None)
    tokens = P(None, ("dp", "shard"), None)
    vector = P(("dp", "shard"))
    placed = (
        tokens,
        rows,
        rows,
        rows,
        vector,
        vector,
        rows,
        rows,
        rows,
        tokens,
        P(None, "dp", "shard", None),
        P(None, "dp", None),
    )
    return jax.shard_map(
        body,
        mesh=mesh,
        in_specs=placed,
        out_specs=(tokens, tokens, rows, rows, rows, vector, vector, rows, rows, rows),
        check_vma=False,
    )
```

```python
import functools

import jax
import jax.numpy as jnp
from jax import lax
from jax.experimental import pallas as pl
from jax.experimental.pallas import tpu as pltpu
from jax.sharding import PartitionSpec as P

EPS = 1e-05
F32 = jnp.float32
BF16 = jnp.bfloat16
LANES = 128


def dot(former, latter, dims, out=F32):
    return lax.dot_general(
        former, latter, ((dims[0], dims[1]), ((), ())), preferred_element_type=F32
    ).astype(out)


def bits_of(count):
    return [1 << k for k in range(count.bit_length() - 1)]


def swap(value, bit, axis="shard"):
    n = lax.axis_size(axis)
    return lax.ppermute(value, axis, [(i, i ^ bit) for i in range(n)])


def route(outer, turn):
    turn = turn % len(outer)
    return outer[turn:] + outer[:turn]


def after(value, *others):
    others = [other for other in others if other is not None]
    if not others:
        return value
    return lax.optimization_barrier((value, *others))[0]


def gather_names(n, parts):
    outer = bits_of(n)[1:]
    names = []
    for m in range(parts):
        order = [0]
        for bit in route(outer, m):
            order = order + [e ^ (bit >> 1) for e in order]
        names.append(order)
    return names


def plane_gather(parts, waits=((), ())):
    n = lax.axis_size("shard")
    outer = bits_of(n)[1:]
    held = [[part] for part in parts]
    steps = []
    for k in range(len(outer)):
        going = [h[0] if len(h) == 1 else jnp.concatenate(h, axis=0) for h in held]
        if k < len(waits):
            going = [after(g, *waits[k]) for g in going]
        came = [swap(going[m], route(outer, m)[k]) for m in range(len(parts))]
        held = [[g, c] for g, c in zip(going, came)]
        steps.append(tuple(came))
    near = [piece for h in held for piece in h]
    far = [swap(piece, 1) for piece in near]
    return near + far, steps


def fold_kernel(rows, plans, *refs):
    count = len(plans)
    kept, came, sends, keeps = (refs[k * count : (k + 1) * count] for k in range(4))
    for m, (going, staying) in enumerate(plans):
        for out, places in ((sends[m], going), (keeps[m], staying)):
            for k, place in enumerate(places):
                at = slice(place * rows, (place + 1) * rows)
                value = kept[m][at, :] + came[m][at, :].astype(F32)
                out[k * rows : (k + 1) * rows, :] = value.astype(out.dtype)


def first_fold_kernel(rows, plans, near, *refs):
    count = len(plans)
    came, sends, keeps = refs[: len(refs) - 2 * count], refs[len(refs) - 2 * count : -count], refs[-count:]
    per = came[0].shape[0] // rows
    for m, (going, staying) in enumerate(plans):
        for out, places in ((sends[m], going), (keeps[m], staying)):
            for k, place in enumerate(places):
                at = slice(place * rows, (place + 1) * rows)
                there = slice(place % per * rows, (place % per + 1) * rows)
                value = near[at, :] + came[place // per][there, :].astype(F32)
                out[k * rows : (k + 1) * rows, :] = value.astype(out.dtype)


def plane_reduce(near, came, parts, wait=(), late=()):
    n = lax.axis_size("shard")
    half = n // 2
    outer = bits_of(n)[1:]
    width = near.shape[1]
    rows = near.shape[0] // (parts * half)
    names = gather_names(n, parts)
    kept, arrived = near, came
    for k in reversed(range(len(outer))):
        plans = []
        for m in range(parts):
            bit = route(outer, m)[k] >> 1
            going = [e for e in names[m] if e & bit]
            base = m * half if kept is near else 0
            plans.append(([base + names[m].index(e) for e in going], [base + names[m].index(e ^ bit) for e in going]))
            names[m] = [e ^ bit for e in going]
        shape = (len(plans[0][0]) * rows, width)
        outs = [(shape, BF16)] * parts + [(shape, F32)] * parts
        if kept is near:
            made = run(functools.partial(first_fold_kernel, rows, plans), outs, [], [near, *came])
            sends = [after(send, *wait) for send in made[:parts]]
        else:
            made = run(functools.partial(fold_kernel, rows, plans), outs, [], [*kept, *arrived])
            sends = [after(send, *late) for send in made[:parts]]
        first = kept is near
        kept = made[parts:]
        arrived = [swap(sends[m], route(outer, m)[k]) for m in range(parts)]
        if first:
            first_came = arrived
    return [*kept, *arrived], first_came


def line_gather(block, waits=((), ())):
    n = lax.axis_size("dp")
    block = after(block, *waits[0])
    first = None
    for bit in reversed(bits_of(n)):
        came = swap(block, bit, "dp")
        first = came if first is None else first
        if bit == 1:
            return block, came, first
        block = after(jnp.concatenate([block, came], axis=1), *waits[1])


def line_reduce(keep, send, wait=()):
    n = lax.axis_size("dp")
    for bit in bits_of(n):
        came = swap(send, bit, "dp")
        if 2 * bit == n:
            return keep, came
        total = keep + came.astype(F32)
        cut = total.shape[0] // 2
        keep, send = total[:cut], after(total[cut:].astype(BF16), *wait)


def reversed_bits(index, n):
    out = 0
    for k, bit in enumerate(bits_of(n)):
        if index & bit:
            out |= n >> (k + 1)
    return out


def turned(value, z, n):
    step = value.shape[-1] // n
    pieces = [value[..., k * step : (k + 1) * step] for k in range(n)]
    out = None
    for k in range(n):
        order = [pieces[k ^ reversed_bits(p, n)] for p in range(n)]
        moved = jnp.concatenate(order, axis=-1)
        out = moved if out is None else jnp.where(z == k, moved, out)
    return out


def exchange(value, z, n, back):
    step = value.shape[1] // n
    pieces = [value[:, p * step : (p + 1) * step] for p in range(n)]

    def reorder(pieces):
        return [pieces[reversed_bits(p, n)] for p in range(n)]

    def flip(pieces):
        for k, bit in enumerate(bits_of(n)):
            low = n >> (k + 1)
            pieces = [jnp.where((z & bit) != 0, pieces[p ^ low], pieces[p]) for p in range(n)]
        return pieces

    return jnp.concatenate(reorder(flip(pieces)) if back else flip(reorder(pieces)), axis=1)


WHOLE = pl.BlockSpec(memory_space=pltpu.VMEM)
SCALAR = pl.BlockSpec(memory_space=pltpu.SMEM)


def run(kernel, outs, scalars, arrays, scratch=()):
    return pl.pallas_call(
        kernel,
        out_shape=[jax.ShapeDtypeStruct(shape, dtype) for shape, dtype in outs],
        in_specs=[SCALAR] * len(scalars) + [WHOLE] * len(arrays),
        out_specs=[WHOLE] * len(outs),
        scratch_shapes=list(scratch),
        compiler_params=pltpu.CompilerParams(vmem_limit_bytes=2 * lax.axis_size("shard") * 2**20),
        cost_estimate=pl.CostEstimate(flops=1000, bytes_accessed=1000, transcendentals=0),
    )(*[jnp.asarray(v, jnp.int32).reshape(1) for v in scalars], *arrays)


def mm(former, latter):
    return lax.dot_general(former, latter, (((1,), (0,)), ((), ())), preferred_element_type=F32)


def mt(former, latter):
    return lax.dot_general(former, latter, (((1,), (1,)), ((), ())), preferred_element_type=F32)


def spread_kernel(n, whole, rest, count, *refs):
    weights, out = refs[:count], refs[count]
    rows = weights[0].shape[0]
    for k in range(count):
        for s in range(n):
            at = slice(k * rows, (k + 1) * rows)
            first = n * whole + s * rest
            out[s, at, :whole] = weights[k][:, s * whole : (s + 1) * whole]
            out[s, at, whole:] = weights[k][:, first : first + rest]


def join_kernel(n, whole, rest, count, came, *refs):
    weights, outs = refs[:count], refs[count:]
    share = whole + rest
    for k in range(count):
        grad, dots = outs[2 * k : 2 * k + 2]
        first = k * share
        tails = [came[s, :, first + whole : first + share] for s in range(n)]
        grad[:, n * whole :] = jnp.concatenate(tails, axis=1).astype(F32)
        for s in range(n):
            grad[:, s * whole : (s + 1) * whole] = came[s, :, first : first + whole].astype(F32)
        dots[...] = jnp.sum(grad[...] * weights[k][...].astype(F32), axis=1, keepdims=True)


def join_in_kernel(n, groups, came, weight, grad, dots):
    rows = came.shape[1]
    for g in range(groups):
        piece = jnp.concatenate([came[s, :, g * rows : (g + 1) * rows] for s in range(n)], axis=1)
        grad[:, g * n * rows : (g + 1) * n * rows] = piece.astype(F32)
    dots[...] = jnp.sum(grad[...] * weight[...].astype(F32), axis=1, keepdims=True)


def by_line(pieces, z, n):
    for k, bit in enumerate(bits_of(n)):
        low = n >> (k + 1)
        pieces = [jnp.where((z & bit) != 0, pieces[p ^ low], pieces[p]) for p in range(n)]
    return [pieces[reversed_bits(p, n)] for p in range(n)]


def out_kernel(n, z, first, second, full, tap_cols):
    rows = first.shape[0] // (n // 2)
    width = full.shape[1]
    pieces = [(first, second)[p // (n // 2)][p % (n // 2) * rows : (p % (n // 2) + 1) * rows, :] for p in range(n)]
    for p, piece in enumerate(by_line(pieces, z[0], n)):
        at = slice(p * rows, (p + 1) * rows)
        full[at, :] = piece[:, :width]
        tap_cols[at, :] = piece[:, width:]


def relative_kernel(n, z, term, conv_term, keep, send):
    rows = term.shape[0] // n
    width = term.shape[1]
    for value, lanes in ((term, slice(0, width)), (conv_term, slice(width, None))):
        pieces = [value[reversed_bits(p, n) * rows : (reversed_bits(p, n) + 1) * rows, :] for p in range(n)]
        for k, bit in enumerate(bits_of(n)):
            low = n >> (k + 1)
            pieces = [jnp.where((z[0] & bit) != 0, pieces[p ^ low], pieces[p]) for p in range(n)]
        for p in range(n):
            out = (keep, send)[p // (n // 2)]
            at = slice(p % (n // 2) * rows, (p % (n // 2) + 1) * rows)
            out[at, lanes] = pieces[p].astype(out.dtype)


def stack_kernel(count, *refs):
    pieces, out = refs[:count], refs[count]
    rows = pieces[0].shape[0]
    for k in range(count):
        out[k * rows : (k + 1) * rows, :] = pieces[k][...]


def product_kernel(former, latter, out):
    out[...] = mm(former[...], latter[...]).astype(out.dtype)


def product(former, latter, blocks):
    rows = former.shape[0] // blocks
    return pl.pallas_call(
        product_kernel,
        out_shape=jax.ShapeDtypeStruct((former.shape[0], latter.shape[1]), BF16),
        grid=(blocks,),
        in_specs=[
            pl.BlockSpec((rows, former.shape[1]), lambda i: (i, 0)),
            pl.BlockSpec(latter.shape, lambda i: (0, 0)),
        ],
        out_specs=pl.BlockSpec((rows, latter.shape[1]), lambda i: (i, 0)),
        compiler_params=pltpu.CompilerParams(vmem_limit_bytes=min(4 * lax.axis_size("shard"), 48) * 2**20),
        cost_estimate=pl.CostEstimate(flops=1000, bytes_accessed=1000, transcendentals=0),
    )(former, latter)


def columns_kernel(chunk, rows, out):
    for k in range(rows.shape[1] // chunk):
        at = slice(k * chunk, (k + 1) * chunk)
        out[at, :] = rows[:, at].astype(F32).T.astype(BF16)


def project_kernel(channels, count, *refs):
    pieces = refs[:count]
    in_a, in_b, own_ref, normed_a, normed_b, product, c_high, c_low, b_out, x_out, own_tok = refs[count : count + 11]
    tok = refs[count + 11]
    rows = pieces[0].shape[0]
    split = in_a.shape[1]
    at_gain = 3 * channels
    gain = jnp.concatenate([in_a[at_gain : at_gain + 1, :], in_b[at_gain : at_gain + 1, :]], axis=1).astype(F32)
    for k in range(0, count, 2):
        at = slice(k * rows, (k + 2) * rows)
        for j in range(2):
            piece = pieces[k + j][...]
            here = slice((k + j) * rows, (k + j + 1) * rows)
            tok[here, :] = piece
            wide = piece.astype(F32)
            unit = wide * lax.rsqrt(jnp.mean(wide * wide, axis=1, keepdims=True) + EPS)
            lean = (unit * gain).astype(BF16)
            normed_a[here, :] = lean[:, :split]
            normed_b[here, :] = lean[:, split:]
        left, right = normed_a[at, :], normed_b[at, :]

        def part(j):
            lines = slice(j * channels, (j + 1) * channels)
            return mt(left, in_a[lines, :]) + mt(right, in_b[lines, :])

        b_part, c_part, x_part = part(0), part(1), part(2)
        high = c_part.astype(BF16)
        product[at, :] = (b_part * x_part).astype(BF16)
        c_high[at, :] = high
        c_low[at, :] = (c_part - high.astype(F32)).astype(BF16)
        b_out[at, :] = b_part
        x_out[at, :] = x_part
    lanes = lax.broadcasted_iota(jnp.int32, (own_ref.shape[0], tok.shape[0]), 1)
    own_tok[...] = mm((own_ref[...] == lanes).astype(F32).astype(BF16), tok[...]).astype(BF16)


def conv_kernel(batches, n, me, product, c_high, c_low, source, offset, taps, p_out, c_out, conv_out, gated_out, gated):
    names = gather_names(n, batches)
    group = source.shape[1]
    half = group // 2
    rows = group // n
    for m in range(batches):
        lanes = lax.broadcasted_iota(jnp.int32, (group, group), 1)
        deal = (source[m] == lanes).astype(F32).astype(BF16)
        first, second = pl.ds(m * half, half), pl.ds((batches + m) * half, half)

        def moved(ref):
            return mm(deal[:, :half], ref[first, :]) + mm(deal[:, half:], ref[second, :])

        wide = moved(product)
        c_part = moved(c_high) + moved(c_low)
        place = offset[m]
        prev_one = jnp.where(place >= 1, pltpu.roll(wide, 1, 0), 0.0)
        prev_two = jnp.where(place >= 2, pltpu.roll(wide, 2, 0), 0.0)
        conv = prev_two * taps[0:1, :] + prev_one * taps[1:2, :] + wide * taps[2:3, :]
        p_out[m] = wide.astype(BF16)
        c_out[m] = c_part
        conv_out[m] = conv
        gated[...] = c_part * conv
        for c in range(2):
            for k, e in enumerate(names[m]):
                other = me[0] ^ (2 * e + c)
                block = gated[pl.ds(pl.multiple_of(other * rows, 8), rows), :]
                at = ((c * batches + m) * (n // 2) + k) * rows
                gated_out[at : at + rows, :] = block.astype(BF16)


def summed(batches, terms):
    return jnp.concatenate([terms[m][...] + terms[batches + m][...].astype(F32) for m in range(batches)], axis=0)


def hidden_kernel(batches, n_dp, z, own_tok, gain, *refs):
    terms, (hidden, unit_out, *parts) = refs[: 2 * batches], refs[2 * batches :]
    value = exchange(own_tok[...].astype(F32), z[0], n_dp, True) + summed(batches, terms)
    hidden[...] = value
    unit = value * lax.rsqrt(jnp.mean(value * value, axis=1, keepdims=True) + EPS)
    unit_out[...] = unit
    lean = (unit * gain[...]).astype(BF16)
    rows = parts[0].shape[0]
    for m in range(batches):
        parts[m][...] = lean[m * rows : (m + 1) * rows]


def gate_kernel(count, *refs):
    pieces = refs[:count]
    two, lean, inner, by_gate, by_up = refs[count:]
    rows = pieces[0].shape[0]
    share = two.shape[0] // 2
    for k in range(0, count, 2):
        at = slice(k * rows, (k + 2) * rows)
        for j in range(2):
            lean[(k + j) * rows : (k + j + 1) * rows, :] = pieces[k + j][...]
        part = lean[at, :]
        gate = mt(part, two[:share, :])
        up = mt(part, two[share:, :])
        sig = jax.nn.sigmoid(gate)
        silu = gate * sig
        inner[at, :] = (silu * up).astype(BF16)
        by_gate[at, :] = (up * sig * (1.0 + gate * (1.0 - sig))).astype(BF16)
        by_up[at, :] = silu.astype(BF16)


def inner_kernel(chunk, cot, down, by_gate, by_up, *refs):
    d_two = refs[-1]
    share = by_gate.shape[1]
    for k in range(cot.shape[0] // chunk):
        at = slice(k * chunk, (k + 1) * chunk)
        d_inner = mt(cot[at, :], down[...])
        d_two[at, :share] = (d_inner * by_gate[at, :].astype(F32)).astype(BF16)
        d_two[at, share:] = (d_inner * by_up[at, :].astype(F32)).astype(BF16)


def inner_half(part, chunk, cot, down, by_gate, by_up, other=None):
    total, share = by_gate.shape

    def rows_of(width):
        return pl.BlockSpec((total // 2, width), lambda i: (part, 0))

    extra = [] if other is None else [other]
    return pl.pallas_call(
        functools.partial(inner_kernel, chunk),
        out_shape=jax.ShapeDtypeStruct((total, 2 * share), BF16),
        grid=(1,),
        in_specs=[rows_of(cot.shape[1]), pl.BlockSpec(down.shape, lambda i: (0, 0)), rows_of(share), rows_of(share)]
        + [pl.BlockSpec(memory_space=pl.ANY)] * len(extra),
        out_specs=rows_of(2 * share),
        input_output_aliases={4: 0} if extra else {},
        compiler_params=pltpu.CompilerParams(vmem_limit_bytes=min(4 * lax.axis_size("shard"), 48) * 2**20),
        cost_estimate=pl.CostEstimate(flops=1000, bytes_accessed=1000, transcendentals=0),
    )(cot, down, by_gate, by_up, *extra)


def rows_kernel(*refs, sides):
    lhs, rhs, outs = refs[0], refs[1 : 1 + sides], refs[1 + sides :]
    rows = outs[0].shape[0]
    per = max(1, 384 // rows)
    step = min(rows, 384)
    for k in range(0, len(outs), per):
        count = min(per, len(outs) - k)
        for first in range(0, rows, step):
            at = slice(k * rows + first, k * rows + first + step * count)
            for j in range(sides):
                split = rhs[j].shape[1]
                value = mm(lhs[at, :], rhs[j][...])
                for piece in range(count):
                    here = value[piece * step : (piece + 1) * step]
                    outs[k + piece][first : first + step, j * split : (j + 1) * split] = here.astype(outs[0].dtype)


def half_rows(lhs, rhs, part, dtype, pieces):
    rows = lhs.shape[0] // 2
    width = sum(side.shape[1] for side in rhs)
    shape = (rows // pieces, width)
    return pl.pallas_call(
        functools.partial(rows_kernel, sides=len(rhs)),
        out_shape=[jax.ShapeDtypeStruct(shape, dtype)] * pieces,
        grid=(1,),
        in_specs=[pl.BlockSpec((rows, lhs.shape[1]), lambda i: (part, 0))]
        + [pl.BlockSpec(side.shape, lambda i: (0, 0)) for side in rhs],
        out_specs=[pl.BlockSpec(shape, lambda i: (0, 0))] * pieces,
        compiler_params=pltpu.CompilerParams(vmem_limit_bytes=min(4 * lax.axis_size("shard"), 48) * 2**20),
        cost_estimate=pl.CostEstimate(flops=1000, bytes_accessed=1000, transcendentals=0),
    )(lhs, *rhs)


def branch_kernel(batches, cot, hidden, unit, gain, *refs):
    terms, parts = refs[: 2 * batches], refs[2 * batches :]
    value = hidden[...]
    inv = lax.rsqrt(jnp.mean(value * value, axis=1, keepdims=True) + EPS)
    scaled = summed(batches, terms) * gain[...]
    one = unit[...]
    mean = jnp.mean(scaled * one, axis=1, keepdims=True)
    lean = (cot[...].astype(F32) + inv * (scaled - one * mean)).astype(BF16)
    rows = parts[0].shape[0]
    for m in range(batches):
        parts[m][...] = lean[m * rows : (m + 1) * rows]


def conv_back_kernel(batches, n, count, me, *refs):
    pieces = refs[:count]
    out_ref, conv, c_nat, p_nat, b_arr, x_arr, source, offset, slot, taps = refs[count : count + 10]
    branch, d_proj, conv_grad, own, natural = refs[count + 10 :]
    channels = taps.shape[1]
    total = branch.shape[0]
    group = total // batches
    half = group // 2
    rows = group // n
    names = gather_names(n, batches)
    for k in range(count):
        size = pieces[k].shape[0]
        branch[k * size : (k + 1) * size, :] = pieces[k][...]
    for c in range(2):
        for m in range(batches):
            k = c * batches + m
            at = slice(k * half, (k + 1) * half)
            gated = mt(branch[at, :], out_ref[...])
            for j, e in enumerate(names[m]):
                other = me[0] ^ (2 * e + c)
                at = m * group + other * rows
                natural[pl.ds(pl.multiple_of(at, 8), rows), :] = gated[j * rows : (j + 1) * rows]
    totals = [jnp.zeros((1, taps.shape[1]), F32)] * 3
    for m in range(batches):
        gated = natural[m * group : (m + 1) * group, :]
        place = offset[m]
        wide = p_nat[m].astype(F32)
        grad = gated * c_nat[m]
        grad_c = (gated * conv[m]).astype(BF16)
        one = jnp.where(place >= 1, grad, 0.0)
        two = jnp.where(place >= 2, grad, 0.0)
        totals[0] += jnp.sum(two * pltpu.roll(wide, 2, 0), axis=0, keepdims=True)
        totals[1] += jnp.sum(one * pltpu.roll(wide, 1, 0), axis=0, keepdims=True)
        totals[2] += jnp.sum(grad * wide, axis=0, keepdims=True)
        d_product = (
            grad * taps[2:3, :]
            + pltpu.roll(one, group - 1, 0) * taps[1:2, :]
            + pltpu.roll(two, group - 2, 0) * taps[0:1, :]
        ).astype(BF16)
        lines = lax.broadcasted_iota(jnp.int32, (group, group), 0)
        undeal = (source[m] == lines).astype(F32).astype(BF16)
        d_prod = mm(undeal, d_product)
        c_back = mm(undeal, grad_c)
        for c in range(2):
            there = pl.ds((c * batches + m) * half, half)
            piece = d_prod[c * half : (c + 1) * half]
            d_proj[there, :channels] = (piece * x_arr[there, :]).astype(BF16)
            d_proj[there, channels : 2 * channels] = c_back[c * half : (c + 1) * half].astype(BF16)
            d_proj[there, 2 * channels :] = (piece * b_arr[there, :]).astype(BF16)
    for k in range(3):
        conv_grad[k : k + 1, :] = totals[k]
    lanes = lax.broadcasted_iota(jnp.int32, (slot.shape[0], total), 1)
    picked = (slot[...] == lanes).astype(F32).astype(BF16)
    own[...] = mm(picked, branch[...]).astype(BF16)


def final_kernel(batches, n_dp, z, tokens, gain, d_hidden, *refs):
    terms, out = refs[:-1], refs[-1]
    back = exchange(summed(batches, terms), z[0], n_dp, True)
    wide = tokens[...].astype(F32)
    inv = lax.rsqrt(jnp.mean(wide * wide, axis=1, keepdims=True) + EPS)
    unit = wide * inv
    scaled = back * gain[...]
    mean = jnp.mean(scaled * unit, axis=1, keepdims=True)
    out[...] = (d_hidden[...].astype(F32) + inv * (scaled - unit * mean)).astype(BF16)


def block_kernel(batches, hidden, *refs):
    terms, out = refs[:-1], refs[-1]
    out[...] = (hidden[...] + summed(batches, terms)).astype(BF16)


def body(
    tokens_in,
    in_weight,
    conv_weight,
    out_weight,
    norm_gain,
    ff_gain,
    gate_weight,
    up_weight,
    down_weight,
    cotangent,
    deal_table,
    seq_lengths,
):
    batches, rows_dev, width = tokens_in.shape
    n, n_dp = lax.axis_size("shard"), lax.axis_size("dp")
    half = n // 2
    me, z = lax.axis_index("shard"), lax.axis_index("dp")
    group = n * rows_dev
    piece_rows = rows_dev // n
    own_rows, hidden_units = gate_weight.shape
    total = batches * group
    outer = bits_of(n)[1:]
    zblock = n * own_rows
    channels = n_dp * own_rows

    whole = hidden_units // (LANES * n) * LANES
    rest = hidden_units // n - whole

    place = jnp.arange(zblock, dtype=jnp.int32)
    identity = (place[:, None] == place[None, :]).astype(BF16)
    own_total = batches * rows_dev
    share = hidden_units // n
    chunk = total // 4
    cut = width // 2
    names = gather_names(n, batches)

    def dealt(blocks):
        return lax.all_to_all(blocks, "shard", split_axis=0, concat_axis=0, tiled=True)

    def flipped(block):
        return dot(block.reshape(zblock, -1), identity, ((0,), (0,)), BF16)

    in_parts = in_weight.reshape(own_rows, 3 * n_dp, n, own_rows).transpose(2, 0, 1, 3)
    in_parts = in_parts.reshape(n, own_rows, 3 * channels)
    spare = 14
    table = deal_table[:, 0, 0, :].astype(BF16).reshape(-1)
    table = jnp.pad(table, (0, own_rows * spare - table.shape[0])).reshape(own_rows, spare)
    extra = jnp.concatenate([norm_gain[:, None], ff_gain[:, None], table], axis=1)
    in_parts = jnp.concatenate([in_parts, jnp.broadcast_to(extra[None], (n,) + extra.shape)], axis=2)
    in_came = dealt(in_parts)
    out_aug = jnp.concatenate(
        [out_weight, conv_weight, jnp.zeros((own_rows, LANES - conv_weight.shape[1]), BF16)], axis=1
    )
    out_lines = out_aug
    out_steps = []
    for bit in reversed(bits_of(n_dp)):
        out_came = swap(out_lines, bit, "dp")
        out_steps.append(out_came)
        if bit > 1:
            out_lines = jnp.concatenate([out_lines, out_came], axis=0)

    tok_turned = turned(after(tokens_in, in_parts), z, n_dp)
    tok_pieces, tok_steps = plane_gather([tok_turned[m] for m in range(batches)], ((), (out_steps[0],)))

    out_full, tap_cols = run(
        functools.partial(out_kernel, n_dp),
        [((channels, width), BF16), ((channels, LANES), BF16)],
        [z],
        [out_lines, out_came],
    )
    taps = tap_cols[:, : conv_weight.shape[1]].astype(F32).T

    deal = in_came[:, :, 3 * channels + 2 :].reshape(n, own_rows * spare)[:, : batches * n]
    deal = deal.reshape(n, batches, n).transpose(1, 0, 2).astype(jnp.int32)
    m_index = jnp.arange(batches, dtype=jnp.int32)[:, None, None, None]
    j_index = jnp.arange(n, dtype=jnp.int32)[None, :, None, None]
    t_index = jnp.arange(piece_rows, dtype=jnp.int32)[None, None, None, :]

    def place_of(e, m):
        out = jnp.zeros_like(e + m)
        for part in range(batches):
            for k, name in enumerate(names[part]):
                out = jnp.where((e == name) & (m == part), k, out)
        return out

    def within(m, holder, row):
        rel = holder ^ me
        return ((rel & 1) * half + place_of(rel >> 1, m)) * rows_dev + row

    def arrival_row(m, holder, row):
        rel = holder ^ me
        return (((rel & 1) * batches + m) * half + place_of(rel >> 1, m)) * rows_dev + row

    slot_row = j_index * piece_rows + t_index
    source = within(m_index, deal[:, :, :, None], slot_row).reshape(batches, group)
    own_deal = lax.dynamic_index_in_dim(deal, me, 1, keepdims=True)[:, :, :, None]
    own_source = arrival_row(m_index, own_deal, me * piece_rows + t_index).reshape(own_total, 1)
    inverse = jnp.sum(jnp.where(deal == me, jnp.arange(n, dtype=jnp.int32)[None, None, :], 0), axis=2)
    slot_source = arrival_row(
        m_index[:, :, 0], j_index[:, :, 0], inverse[:, :, None] * piece_rows + t_index[:, 0]
    ).reshape(own_total, 1)

    lengths = seq_lengths[:, 0, :]
    places = jnp.arange(group, dtype=jnp.int32)
    seq_start = jnp.zeros((batches, group), jnp.int32)
    start = jnp.zeros((batches,), jnp.int32)
    for k in range(lengths.shape[1]):
        seq_start = jnp.where(start[:, None] <= places[None, :], start[:, None], seq_start)
        start = start + lengths[:, k]
    offset = (places[None, :] - seq_start)[:, :, None]

    waits = (*tok_pieces, out_full, taps, source, own_source, slot_source, offset)
    in_a, in_b, in_first = line_gather(flipped(in_came), ((), waits))

    def spread(*weights):
        rows = sum(weight.shape[0] for weight in weights)
        kernel = functools.partial(spread_kernel, n, whole, rest, len(weights))
        return run(kernel, [((n, rows, share), BF16)], [], weights)[0]

    ff_came = dealt(after(spread(gate_weight, up_weight), in_first, *tok_steps[-1]))
    gate_block, up_block = [flipped(ff_came[:, k * own_rows : (k + 1) * own_rows]) for k in range(2)]
    two_block = after(jnp.concatenate([gate_block, up_block], axis=0), in_b)
    down_came = dealt(after(spread(down_weight), ff_came))
    two = lax.all_gather(two_block, "dp", axis=1, tiled=True)

    def natural_row(row):
        both = jnp.concatenate([in_a[row : row + 1], in_b[row : row + 1]], axis=1)
        step = width // n_dp
        out = None
        for k in range(n_dp):
            order = [reversed_bits(k ^ p, n_dp) for p in range(n_dp)]
            moved = jnp.concatenate([both[:, q * step : (q + 1) * step] for q in order], axis=1)
            out = moved if out is None else jnp.where(z == k, moved, out)
        return out.astype(F32)

    gain_one = natural_row(3 * channels)
    gain_two = natural_row(3 * channels + 1)
    arr = (total, channels)
    nat = (batches, group, channels)
    own = (own_total, width)
    side = (total, cut)
    normed_a, normed_b, made, c_high, c_low, b_arr, x_arr, own_tok = run(
        functools.partial(project_kernel, channels, len(tok_pieces)),
        [(side, BF16), (side, BF16), (arr, BF16), (arr, BF16), (arr, BF16), (arr, F32), (arr, F32), (own, BF16)],
        [],
        [*tok_pieces, in_a, in_b, own_source],
        [pltpu.VMEM((total, width), BF16)],
    )
    p_nat, c_nat, conv_out, gated_arr = run(
        functools.partial(conv_kernel, batches, n),
        [(nat, BF16), (nat, F32), (nat, F32), (arr, BF16)],
        [me],
        [made, c_high, c_low, source[:, :, None], offset, taps],
        [pltpu.VMEM((group, channels), F32)],
    )
    down_block = flipped(after(down_came, gated_arr))
    down = lax.all_gather(down_block, "dp", axis=1, tiled=True)
    cot_pieces, cot_steps = plane_gather([cotangent[m] for m in range(batches)], ((ff_came, *tok_steps[-1]), ()))

    def summed_rows(lhs, rhs, wait=()):
        far = half_rows(lhs, rhs, 1, BF16, 2 * batches)
        [near] = half_rows(lhs, rhs, 0, F32, 1)
        return plane_reduce(near, [swap(piece, 1) for piece in far], batches, wait)[0]

    mine = ((rows_dev, width), BF16)
    hidden, unit_two, *ff_own = run(
        functools.partial(hidden_kernel, batches, n_dp),
        [(own, F32), (own, F32)] + [mine] * batches,
        [z],
        [own_tok, gain_two, *summed_rows(gated_arr, [out_full], (*cot_steps[-1], down_came))],
    )
    ff_pieces, ff_steps = plane_gather(ff_own)
    whole_rows = ((total, width), BF16)
    [cot_all] = run(functools.partial(stack_kernel, len(cot_pieces)), [whole_rows], [], cot_pieces)

    ff = (total, share)
    lean, ff_inner, by_gate, by_up = run(
        functools.partial(gate_kernel, len(ff_pieces)),
        [whole_rows, (ff, BF16), (ff, BF16), (ff, BF16)],
        [],
        [*ff_pieces, two],
    )

    def line_sum(former, latter, wait=()):
        value = after(product(former, latter, 4), *wait)
        return lax.psum_scatter(value, "dp", scatter_dimension=0, tiled=True)

    turn = functools.partial(columns_kernel, width // 6)
    [cot_columns] = run(turn, [((width, total), BF16)], [], [cot_all])
    [lean_columns] = run(turn, [((width, total), BF16)], [], [lean])
    down_sum = line_sum(cot_columns, ff_inner)
    d_far = inner_half(1, chunk, after(cot_all, lean_columns), down, by_gate, by_up)
    far = half_rows(d_far, [two], 1, BF16, 2 * batches)
    came = [swap(piece, 1) for piece in far]
    d_two = inner_half(0, chunk, after(cot_all, *far), down, by_gate, by_up, d_far)
    [near] = half_rows(after(d_two, *came), [two], 0, F32, 1)
    d_ff, first_came = plane_reduce(near, came, batches)
    two_sum = line_sum(lean_columns, d_two, first_came)
    cot_own = cotangent.reshape(own)
    branch_own = run(
        functools.partial(branch_kernel, batches),
        [mine] * batches,
        [],
        [cot_own, hidden, unit_two, gain_two, *d_ff],
    )
    block_came = [swap(piece, 1) for piece in half_rows(ff_inner, [down], 1, BF16, 2 * batches)]
    [block_near] = half_rows(ff_inner, [down], 0, F32, 1)
    branch_pieces, branch_steps = plane_gather(branch_own, ((), (block_near,)))
    block_sum, block_first = plane_reduce(block_near, block_came, batches, branch_steps[-1])


    branch, d_proj, conv_term, d_hidden_own = run(
        functools.partial(conv_back_kernel, batches, n, len(branch_pieces)),
        [whole_rows, ((total, 3 * channels), BF16), ((3, channels), F32), (own, BF16)],
        [me],
        [
            *branch_pieces,
            out_full,
            conv_out,
            c_nat,
            p_nat,
            b_arr,
            x_arr,
            source[:, None, :],
            offset,
            slot_source,
            taps,
        ],
        [pltpu.VMEM((total, channels), F32)],
    )
    in_sides = [in_a[: 3 * channels], in_b[: 3 * channels]]
    down_back = dealt(after(down_sum, *branch_steps[-1]).reshape(n, own_rows, -1))
    far = half_rows(after(d_proj, *block_first), in_sides, 1, BF16, 2 * batches)
    [near] = half_rows(d_proj, in_sides, 0, F32, 1)
    d_normed, _ = plane_reduce(
        near, [swap(piece, 1) for piece in far], batches, (down_back, *block_sum[batches:])
    )
    [block_out] = run(functools.partial(block_kernel, batches), [(own, BF16)], [], [hidden, *block_sum])
    block_out = block_out.reshape(tokens_in.shape)
    [tokens_grad] = run(
        functools.partial(final_kernel, batches, n_dp),
        [(own, BF16)],
        [z],
        [tokens_in.reshape(own), gain_one, d_hidden_own, *d_normed],
    )
    tokens_grad = tokens_grad.reshape(tokens_in.shape)

    conv_cols = jnp.pad(conv_term.T, ((0, 0), (0, LANES - conv_term.shape[0])))
    keep, send = run(
        functools.partial(relative_kernel, n_dp),
        [((channels // 2, width + LANES), F32), ((channels // 2, width + LANES), BF16)],
        [z],
        [dot(gated_arr, branch, ((0,), (0,))), conv_cols],
    )
    out_came = []
    for bit in bits_of(n_dp):
        came = swap(send, bit, "dp")
        out_came.append(came)
        keep = keep + came.astype(F32)
        if 2 * bit < n_dp:
            keep, send = jnp.split(keep, 2, axis=0)
            send = after(send.astype(BF16), *d_normed[batches:])
    in_sum = line_reduce(dot(normed_a, d_proj, ((0,), (0,))), dot(normed_b, d_proj, ((0,), (0,)), BF16), (*d_normed[batches:], out_came[0]))
    out_grad = keep[:, :width]
    conv_grad = keep[:, width : width + conv_weight.shape[1]]
    two_back = dealt(two_sum.reshape(n, own_rows, -1))
    in_total = (in_sum[0] + in_sum[1].astype(F32)).astype(BF16).reshape(n, own_rows, -1)
    in_back = dealt(after(in_total, two_back))

    def joined(kernel, came, *weights):
        outs = [((own_rows, 1), F32)] * (2 * len(weights))
        outs[::2] = [(weight.shape, F32) for weight in weights]
        return run(kernel, outs, [], [came, *weights])

    join = functools.partial(join_kernel, n, whole, rest)
    down_grad, _ = joined(functools.partial(join, 1), down_back, down_weight)
    gate_grad, gate_dots, up_grad, up_dots = joined(functools.partial(join, 2), two_back, gate_weight, up_weight)
    in_grad, in_dots = joined(functools.partial(join_in_kernel, n, 3 * n_dp), in_back, in_weight)
    norm_gain_grad = in_dots[:, 0] / norm_gain.astype(F32)
    ff_gain_grad = (gate_dots + up_dots)[:, 0] / ff_gain.astype(F32)
    return (
        block_out,
        tokens_grad,
        in_grad,
        conv_grad,
        out_grad,
        norm_gain_grad,
        ff_gain_grad,
        gate_grad,
        up_grad,
        down_grad,
    )


def solution(mesh):
    rows = P(("dp", "shard"), None)
    tokens = P(None, ("dp", "shard"), None)
    vector = P(("dp", "shard"))
    placed = (
        tokens,
        rows,
        rows,
        rows,
        vector,
        vector,
        rows,
        rows,
        rows,
        tokens,
        P(None, "dp", "shard", None),
        P(None, "dp", None),
    )
    return jax.shard_map(
        body,
        mesh=mesh,
        in_specs=placed,
        out_specs=(tokens, tokens, rows, rows, rows, vector, vector, rows, rows, rows),
        check_vma=False,
    )
```
